256 devices in a mesh: roll: 32 (over z, y_lo, core), kv: 8 (over y_hi, x).
Axes of the slice: x: 4, y: 4 (y_hi: 2, y_lo: 2; y = y_hi * 2 + y_lo), z: 8, core: 2. Of those that a mesh axis runs over, the one named last changes fastest.
Arguments:
- prompt_q: bfloat16 [2048, 8192], P('roll', 'kv'), may hold values from -144 to 144
- prompt_k: bfloat16 [2048, 1024], P('roll', 'kv'), may hold values from -6 to 6
- prompt_v: bfloat16 [2048, 1024], P('roll', 'kv'), may hold values from -6 to 6
- prompt_do: bfloat16 [2048, 8192], P('roll', 'kv'), may hold values from -6 to 6
- suffix_q: bfloat16 [32, 256, 8192], P('roll', None, 'kv'), may hold values from -144 to 144
- suffix_k: bfloat16 [32, 256, 1024], P('roll', None, 'kv'), may hold values from -6 to 6
- suffix_v: bfloat16 [32, 256, 1024], P('roll', None, 'kv'), may hold values from -6 to 6
- suffix_do: bfloat16 [32, 256, 8192], P('roll', None, 'kv'), may hold values from -6 to 6
- lengths: int32 [32], P('roll'), may hold values from 128 to 256, as said below
- key_weight: bfloat16 [8192, 1024], P(None, 'kv'), may hold values from -0.1875 to 0.1875
- value_weight: bfloat16 [8192, 1024], P(None, 'kv'), may hold values from -0.1875 to 0.1875
Outputs:
- prompt_dq: bfloat16 [2048, 8192], P('roll', 'kv')
- prompt_dk: bfloat16 [2048, 1024], P('roll', 'kv')
- prompt_dv: bfloat16 [2048, 1024], P('roll', 'kv')
- suffix_dq: bfloat16 [32, 256, 8192], P('roll', None, 'kv')
- suffix_dk: bfloat16 [32, 256, 1024], P('roll', None, 'kv')
- suffix_dv: bfloat16 [32, 256, 1024], P('roll', None, 'kv')
- input_grad: bfloat16 [2048, 8192], P(('roll', 'kv'))
The draws below stay inside these ranges and needn't reach their ends.
Inputs may be any that keep to these rules, and one draw needn't show every extreme that they name: `lengths`: multiples of 128; some rollout has 256.
All inputs are finite; a program needn't handle non-finite values.
Results may differ from the reference program's by a relative error of at most 0.0057.
Values may be sent and summed in bfloat16 or wider, within the bound.
A program may use at most 64 MiB of HBM per device.

```python
import jax
import jax.numpy as jnp
from jax import lax

D = 8192
QH = 64
KVH = 8
HD = 128
S = 256
BLOCK = 128
P_SIZE = 2048
ROLLOUTS = 32


def prompt_keys(key):
    return jnp.clip(jax.random.normal(key, (P_SIZE, KVH * HD), jnp.float32), -6.0, 6.0)


def draw_prompt_k(key, part):
    return prompt_keys(key).astype(jnp.bfloat16)


def draw_prompt_q(key, part):
    key = jax.random.fold_in(key, 3)
    values = jnp.clip(jax.random.normal(key, (P_SIZE, QH * HD), jnp.float32), -6.0, 6.0)
    return values.astype(jnp.bfloat16)


def draw_suffix_q(key, part):
    key = jax.random.fold_in(key, 4)
    values = jnp.clip(jax.random.normal(key, (ROLLOUTS * S, QH * HD), jnp.float32), -6.0, 6.0)
    return values.reshape(ROLLOUTS, S, QH * HD).astype(jnp.bfloat16)


def draw_lengths(key, part):
    key = jax.random.fold_in(key, 5)
    counts = jax.random.randint(key, (ROLLOUTS,), 1, S // BLOCK + 1)
    longest = jax.random.randint(jax.random.fold_in(key, 6), (), 0, ROLLOUTS)
    counts = counts.at[longest].set(S // BLOCK)
    return (counts * BLOCK).astype(jnp.int32)


def level_of(key, shape, cuts, smallest, top_value):
    loudness = 1.0
    for dim, blocks in cuts:
        heights = jax.random.uniform(jax.random.fold_in(jax.random.fold_in(key, 6), dim), (blocks,), jnp.float32, smallest / len(cuts), top_value / len(cuts))
        loudness = loudness * jnp.repeat(jnp.exp(heights), shape[dim] // blocks).reshape((-1,) + (1,) * (len(shape) - 1 - dim))
    return loudness


def noise(stream_key, shape, width, reach, split=(), held_as=jnp.bfloat16):
    loudness = level_of(stream_key, shape, split, -0.22, 0.18) if split else 1.0
    drawn = jax.random.normal(stream_key, shape, jnp.float32) * width * loudness
    return jnp.minimum(jnp.maximum(drawn, -reach), reach).astype(held_as)


def setup_inputs(seed: int = 0) -> dict:
    seeds = jax.random.split(jax.random.key(seed), 12)
    prompt_q = draw_prompt_q(jax.random.fold_in(seeds[11], 71), 0)
    prompt_k = draw_prompt_k(jax.random.fold_in(seeds[11], 71), 0)
    prompt_v = noise(seeds[2], (P_SIZE, KVH * HD), 1.0, 6.0, ((0, 32), (1, 8)))
    prompt_do = noise(seeds[3], (P_SIZE, QH * HD), 1.0, 6.0, ((0, 32), (1, 8)))
    suffix_q = draw_suffix_q(jax.random.fold_in(seeds[11], 71), 0)
    suffix_k = noise(seeds[5], (ROLLOUTS, S, KVH * HD), 1.0, 6.0, ((0, 32), (2, 8)))
    suffix_v = noise(seeds[6], (ROLLOUTS, S, KVH * HD), 1.0, 6.0, ((0, 32), (2, 8)))
    suffix_do = noise(seeds[7], (ROLLOUTS, S, QH * HD), 1.0, 6.0, ((0, 32), (2, 8)))
    lengths = draw_lengths(jax.random.fold_in(seeds[11], 71), 0)
    key_weight = noise(seeds[9], (D, KVH * HD), (KVH * HD) ** -0.5, 0.1875, ((1, 8),))
    value_weight = noise(seeds[10], (D, KVH * HD), (KVH * HD) ** -0.5, 0.1875, ((1, 8),))
    return {"prompt_q": prompt_q, "prompt_k": prompt_k, "prompt_v": prompt_v, "prompt_do": prompt_do, "suffix_q": suffix_q, "suffix_k": suffix_k, "suffix_v": suffix_v, "suffix_do": suffix_do, "lengths": lengths, "key_weight": key_weight, "value_weight": value_weight}


neg_big = -1e+30

def rounded(values):
    return lax.optimization_barrier(values.astype(jnp.bfloat16)).astype(jnp.float32)

def softgrad(score, dprob, allowed):
    masked = jnp.where(allowed, score, neg_big)
    top = lax.optimization_barrier(jnp.max(masked, axis=-1, keepdims=True))
    expo = jnp.where(allowed, jnp.exp(masked - top), 0.0)
    logsum = top + jnp.log(lax.optimization_barrier(jnp.sum(expo, axis=-1, keepdims=True)))
    prob = jnp.where(allowed, jnp.exp(masked - logsum), 0.0)
    delta = lax.optimization_barrier(jnp.sum(prob * dprob, axis=-1, keepdims=True))
    return (rounded(prob * (dprob - delta)), rounded(prob))

def reference(prompt_q, prompt_k, prompt_v, prompt_do, suffix_q, suffix_k, suffix_v, suffix_do, lengths, key_weight, value_weight):
    scale = HD ** (-0.5)
    group = QH // KVH
    f32 = jnp.float32
    pq = prompt_q.astype(f32).reshape(P_SIZE, KVH, group, HD).transpose(1, 0, 2, 3)
    pdo = prompt_do.astype(f32).reshape(P_SIZE, KVH, group, HD).transpose(1, 0, 2, 3)
    pk = prompt_k.astype(f32).reshape(P_SIZE, KVH, HD).transpose(1, 0, 2)
    pv = prompt_v.astype(f32).reshape(P_SIZE, KVH, HD).transpose(1, 0, 2)
    position = jnp.arange(S, dtype=jnp.int32)
    live = position[None, :] < lengths[:, None]
    sq = suffix_q.astype(f32).reshape(ROLLOUTS, S, KVH, group, HD).transpose(2, 0, 1, 3, 4)
    sdo = jnp.where(live[:, :, None], suffix_do, jnp.zeros_like(suffix_do)).astype(f32)
    sdo = sdo.reshape(ROLLOUTS, S, KVH, group, HD).transpose(2, 0, 1, 3, 4)
    sk = suffix_k.astype(f32).reshape(ROLLOUTS, S, KVH, HD).transpose(2, 0, 1, 3)
    sv = suffix_v.astype(f32).reshape(ROLLOUTS, S, KVH, HD).transpose(2, 0, 1, 3)
    prompt_pos = jnp.arange(P_SIZE, dtype=jnp.int32)
    causal = prompt_pos[None, :] <= prompt_pos[:, None]
    self_ok = (position[None, None, :] <= position[None, :, None]) & (position[None, None, :] < lengths[:, None, None])

    def one_head(items):
        q_p, do_p, k_p, v_p, q_s, do_s, k_s, v_s = items
        score = jnp.einsum('rgd,nd->grn', q_p, k_p) * scale
        dprob = jnp.einsum('rgd,nd->grn', do_p, v_p)
        dscore, probh = softgrad(score, dprob, causal[None])
        dq_p = jnp.einsum('grn,nd->rgd', dscore, k_p) * scale
        dk_p = jnp.einsum('grn,rgd->nd', dscore, q_p)
        dv_p = jnp.einsum('grn,rgd->nd', probh, do_p)

        def one_roll(carry, parts):
            q, do, k, v, allowed_self = parts
            keys = jnp.concatenate([k_p, k], axis=0)
            vals = jnp.concatenate([v_p, v], axis=0)
            allowed = jnp.concatenate([jnp.ones((S, P_SIZE), bool), allowed_self], axis=1)[None]
            sc = jnp.einsum('rgd,nd->grn', q, keys) * scale
            dp = jnp.einsum('rgd,nd->grn', do, vals)
            ds, pb = softgrad(sc, dp, allowed)
            dq = jnp.einsum('grn,nd->rgd', ds, keys) * scale
            dkk = jnp.einsum('grn,rgd->nd', ds, q)
            dvv = jnp.einsum('grn,rgd->nd', pb, do)
            return ((carry[0] + dkk[:P_SIZE], carry[1] + dvv[:P_SIZE]), (dq, dkk[P_SIZE:] * scale, dvv[P_SIZE:]))
        (dk_all, dv_all), (dq_s, dk_s, dv_s) = lax.scan(one_roll, (dk_p, dv_p), (q_s, do_s, k_s, v_s, self_ok))
        return (dq_p, dk_all * scale, dv_all, dq_s, dk_s, dv_s)
    dq_p, dk_p, dv_p, dq_s, dk_s, dv_s = lax.map(one_head, (pq, pdo, pk, pv, sq, sdo, sk, sv))
    dk_round = dk_p.astype(jnp.bfloat16)
    dv_round = dv_p.astype(jnp.bfloat16)
    kw = key_weight.astype(f32).reshape(D, KVH, HD)
    vw = value_weight.astype(f32).reshape(D, KVH, HD)
    input_grad = jnp.einsum('hnd,xhd->nx', dk_round.astype(f32), kw) + jnp.einsum('hnd,xhd->nx', dv_round.astype(f32), vw)
    prompt_dq = dq_p.transpose(1, 0, 2, 3).reshape(P_SIZE, QH * HD).astype(jnp.bfloat16)
    prompt_dk = dk_round.transpose(1, 0, 2).reshape(P_SIZE, KVH * HD)
    prompt_dv = dv_round.transpose(1, 0, 2).reshape(P_SIZE, KVH * HD)
    suffix_dq = dq_s.transpose(1, 2, 0, 3, 4).reshape(ROLLOUTS, S, QH * HD).astype(jnp.bfloat16)
    suffix_dk = dk_s.transpose(1, 2, 0, 3).reshape(ROLLOUTS, S, KVH * HD).astype(jnp.bfloat16)
    suffix_dv = dv_s.transpose(1, 2, 0, 3).reshape(ROLLOUTS, S, KVH * HD).astype(jnp.bfloat16)
    return (prompt_dq, prompt_dk, prompt_dv, suffix_dq, suffix_dk, suffix_dv, input_grad.astype(jnp.bfloat16))
```

```python
import functools

import jax
import jax.numpy as jnp
from jax import lax
from jax.experimental import pallas as pl
from jax.experimental.pallas import tpu as pltpu
from jax.sharding import PartitionSpec as P

F32 = jnp.float32
BF = jnp.bfloat16
HD = 128
HEADS = 8
PR = 64
SR = 256
ROLL = 32
KEYS = 2048
CK = 256
SCALE = HD**-0.5
ALPHA = SCALE * 1.4426950408889634
NEG = -1e30
NT = (((1,), (1,)), ((), ()))
NN = (((1,), (0,)), ((), ()))
MESH = pl.DeviceIdType.MESH
D = 8192
NCOL = 4
CW = D // 2 // NCOL
HW = CW // 2


def dot(a, b, dims):
    return lax.dot_general(a, b, dims, preferred_element_type=F32)


def fold(x, op):
    return op(x.reshape(x.shape[0] // 8, 8, x.shape[1]), axis=0)


def body_kernel(
    pq, pk, pv, pdo, sq, sk, sv, sdo, ln, kw_hbm, vw_hbm,
    o_pdq, o_pdk, o_pdv, o_sdq, o_sdk, o_sdv, o_in,
    kv, kt, q, do, ex, dsc, dp_s, s_s, kw, vw,
    a_send, a_keep, a_recv, b_send, b_keep, b_recv, c_send, c_recv,
    part, x1_send, x1_recv, x2_send, x2_recv, y_keep, y_send, y_recv,
    loc, ag_s, ag_r, a_ss, a_rs, b_ss, b_rs, c_ss, c_rs,
    x1_ss, x1_rs, x2_ss, x2_rs, y_ss, y_rs,
):
    roll = lax.axis_index("roll")
    grp = lax.axis_index("kv")
    z = roll // 4
    y = (roll // 2) % 2
    c = roll % 2
    yh = grp // 4
    x = grp % 4

    def rdev(zz, yy, cc):
        return (zz * 4 + yy * 2 + cc, grp)

    def kdev(hh, xx):
        return (roll, hh * 4 + xx)

    sib = rdev(z, y, 1 - c)
    ypar = rdev(z, 1 - y, c)
    xp = kdev(yh, (x + 1) % 4)
    xm = kdev(yh, (x + 3) % 4)
    hpar = kdev(1 - yh, x)

    copies = []

    def local(src, dst):
        cp = pltpu.make_async_copy(src, dst, loc.at[len(copies)])
        cp.start()
        copies.append(cp)

    local(pk, kv.at[roll, 0])
    local(pv, kv.at[roll, 1])
    for h in range(HEADS):
        cols = slice(h * HD, (h + 1) * HD)
        local(sq.at[0, :, cols], q.at[h * SR : (h + 1) * SR, :])
        local(sdo.at[0, :, cols], do.at[h * SR : (h + 1) * SR, :])
        base = HEADS * SR + h * PR
        local(pq.at[:, cols], q.at[base : base + PR, :])
        local(pdo.at[:, cols], do.at[base : base + PR, :])
    for i in range(4):
        local(sk.at[0, i * PR : (i + 1) * PR, :], kv.at[ROLL + i, 0])
        local(sv.at[0, i * PR : (i + 1) * PR, :], kv.at[ROLL + i, 1])
    local(kw_hbm, kw)
    local(vw_hbm, vw)

    barrier = pltpu.get_barrier_semaphore()
    peers = [rdev((z + d) % 8, y, c) for d in range(1, 8)] + [sib, ypar, xp, xm, hpar]
    for peer in peers:
        pl.semaphore_signal(barrier, inc=1, device_id=peer, device_id_type=MESH)
    pl.semaphore_wait(barrier, len(peers))

    def gather_copy(block, peer, slot):
        return pltpu.make_async_remote_copy(
            src_ref=kv.at[block], dst_ref=kv.at[block],
            send_sem=ag_s.at[slot], recv_sem=ag_r.at[block],
            device_id=peer, device_id_type=MESH,
        )

    sends = []

    def push(block, peer):
        cp = gather_copy(block, peer, len(sends))
        cp.start()
        sends.append(cp)

    copies[0].wait()
    copies[1].wait()
    order = (1, 7, 2, 6, 3, 5, 4)
    for d in order:
        push(roll, rdev((z + d) % 8, y, c))
    push(roll, ypar)
    push(roll, sib)
    for d in order:
        src = ((z + 8 - d) % 8) * 4 + y * 2 + c
        gather_copy(src, sib, 0).wait_recv()
        push(src, ypar)
        push(src, sib)
    for d in (0,) + order:
        src = ((z + 8 - d) % 8) * 4 + (1 - y) * 2 + c
        gather_copy(src, sib, 0).wait_recv()
        push(src, sib)
    for cp in copies[2:-2]:
        cp.wait()
    for d in (0,) + order:
        for yy in range(2):
            src = ((z + 8 - d) % 8) * 4 + yy * 2 + 1 - c
            gather_copy(src, sib, 0).wait_recv()
    for cp in sends:
        cp.wait_send()

    def keys(i):
        return kv[4 * i : 4 * i + 4, 0].reshape(CK, HD)

    def values(i):
        return kv[4 * i : 4 * i + 4, 1].reshape(CK, HD)

    n_live = ln[0]
    for i in range(9):
        kt[:, i * CK : (i + 1) * CK] = keys(i).T
    live = lax.broadcasted_iota(jnp.int32, (SR, HD), 0) < n_live
    for h in range(HEADS):
        rows = slice(h * SR, (h + 1) * SR)
        do[rows, :] = jnp.where(live, do[rows, :], jnp.zeros((), BF))
    kpos = lax.broadcasted_iota(jnp.int32, (CK, SR), 0)
    qpos = lax.broadcasted_iota(jnp.int32, (CK, SR), 1)

    def own_mask(i, s):
        if i < 8:
            return s
        return jnp.where((kpos <= qpos) & (kpos < n_live), s, NEG)

    def causal_mask(i, s):
        return jnp.where(kpos + i * CK <= roll * PR + (qpos & (PR - 1)), s, NEG)

    def tile(t, chunks, mask):
        r0 = pl.multiple_of(t * SR, SR)
        cols = pl.ds(r0, SR)
        qt = q[cols, :]
        dt = do[cols, :]
        top = jnp.full((8, SR), NEG, F32)
        for i in range(chunks):
            s = mask(i, dot(keys(i), qt, NT))
            s_s[i * CK : (i + 1) * CK, :] = s
            top = jnp.maximum(top, fold(s, jnp.max))
        top = jnp.max(top, axis=0, keepdims=True) * ALPHA
        total = jnp.zeros((8, SR), F32)
        delta = jnp.zeros((8, SR), F32)
        for i in range(chunks):
            rows = slice(i * CK, (i + 1) * CK)
            e = jnp.exp2(s_s[rows, :] * ALPHA - top)
            dp = dot(values(i), dt, NT)
            total = total + fold(e, jnp.sum)
            delta = delta + fold(e * dp, jnp.sum)
            ex[rows, cols] = e.astype(BF)
            dp_s[rows, :] = dp
        inv = 1.0 / jnp.sum(total, axis=0, keepdims=True)
        delta = jnp.sum(delta, axis=0, keepdims=True) * inv
        acc = jnp.zeros((HD, SR), F32)
        for i in range(chunks):
            rows = slice(i * CK, (i + 1) * CK)
            ds = (ex[rows, cols].astype(F32) * (dp_s[rows, :] - delta)).astype(BF)
            dsc[rows, cols] = ds
            acc = acc + dot(kt[:, rows], ds, NN)
        invc = jnp.broadcast_to(inv, (HD, SR)).T
        q[cols, :] = (qt.astype(F32) * invc).astype(BF)
        do[cols, :] = (dt.astype(F32) * invc).astype(BF)
        return (acc * (inv * SCALE)).T.astype(BF)

    def roll_tile(t, carry):
        o_sdq[0, :, pl.ds(pl.multiple_of(t * HD, HD), HD)] = tile(t, 9, own_mask)
        return carry

    lax.fori_loop(0, HEADS, roll_tile, 0)

    def prompt_tile(t, carry):
        dq = tile(t, 8, causal_mask)
        for h in range(4):
            col = pl.multiple_of(((t - HEADS) * 4 + h) * HD, HD)
            o_pdq[:, pl.ds(col, HD)] = dq[h * PR : (h + 1) * PR, :]
        return carry

    lax.fori_loop(HEADS, HEADS + 2, prompt_tile, 0)

    own = slice(KEYS, KEYS + SR)
    live_rows = HEADS * SR

    def zoff(i):
        return (z + 4 + (1 - 2 * (i % 2)) * ((i + 1) // 2)) % 8

    def a_copy(i):
        return pltpu.make_async_remote_copy(
            src_ref=a_send.at[i], dst_ref=a_recv.at[i], send_sem=a_ss.at[i],
            recv_sem=a_rs.at[i], device_id=sib, device_id_type=MESH,
        )

    def b_copy(i):
        return pltpu.make_async_remote_copy(
            src_ref=b_send.at[i], dst_ref=b_recv.at[i], send_sem=b_ss.at[i],
            recv_sem=b_rs.at[i], device_id=ypar, device_id_type=MESH,
        )

    def c_copy(i, slot, zz):
        return pltpu.make_async_remote_copy(
            src_ref=c_send.at[i], dst_ref=c_recv.at[slot], send_sem=c_ss.at[i],
            recv_sem=c_rs.at[slot], device_id=rdev(zz, y, c), device_id_type=MESH,
        )

    first_core = c == 0
    first_y = y == 0

    def compute(i):
        k0 = pl.multiple_of(zoff(i) * CK, CK)
        dk = dot(dsc[pl.ds(k0, CK), :], q[...], NN)
        dv = dot(ex[pl.ds(k0, CK), :], do[...], NN)
        for yy in range(2):
            lo = slice(yy * 2 * PR, yy * 2 * PR + PR)
            hi = slice(yy * 2 * PR + PR, yy * 2 * PR + 2 * PR)
            for part_, g in ((0, dk), (1, dv)):
                col = slice(part_ * HD, (part_ + 1) * HD)
                a_keep[i, yy, :, col] = jnp.where(first_core, g[lo], g[hi])
                a_send[i, yy, :, col] = jnp.where(first_core, g[hi], g[lo]).astype(BF)
        a_copy(i).start()

    def after_a(i):
        a_copy(i).wait_recv()
        s0 = a_keep[i, 0] + a_recv[i, 0].astype(F32)
        s1 = a_keep[i, 1] + a_recv[i, 1].astype(F32)
        b_keep[i] = jnp.where(first_y, s0, s1)
        b_send[i] = jnp.where(first_y, s1, s0).astype(BF)
        b_copy(i).start()

    def after_b(i):
        b_copy(i).wait_recv()
        return b_keep[i] + b_recv[i].astype(F32)

    def send_c(i):
        c_send[i] = after_b(i).astype(BF)
        c_copy(i, z, zoff(i)).start()

    def grads(i, carry):
        compute(i)

        @pl.when(i >= 1)
        def _():
            after_a(i - 1)

        @pl.when(i >= 2)
        def _():
            send_c(i - 2)

        return carry

    lax.fori_loop(0, 8, grads, 0)
    after_a(7)
    send_c(6)
    o_sdv[0] = dot(ex[own, 0:live_rows], do[0:live_rows, :], NN).astype(BF)
    o_sdk[0] = (dot(dsc[own, 0:live_rows], q[0:live_rows, :], NN) * SCALE).astype(BF)
    summed = after_b(7)
    for d in (1, 7, 2, 6, 3, 5, 4):
        slot = (z + d) % 8
        c_copy(0, slot, slot).wait_recv()
        summed = summed + c_recv[slot].astype(F32)
    dk = (summed[:, :HD] * SCALE).astype(BF)
    dv = summed[:, HD:].astype(BF)
    o_pdk[...] = dk
    o_pdv[...] = dv
    for i in range(8):
        a_copy(i).wait_send()
        b_copy(i).wait_send()
    for i in range(7):
        c_copy(i, z, zoff(i)).wait_send()
    copies[-2].wait()
    copies[-1].wait()

    def x_copy(send, recv, ss, rs, k, side):
        return pltpu.make_async_remote_copy(
            src_ref=send.at[k, side], dst_ref=recv.at[k, side], send_sem=ss.at[k, side],
            recv_sem=rs.at[k, side], device_id=(xp, xm)[side], device_id_type=MESH,
        )

    def y_copy(k):
        return pltpu.make_async_remote_copy(
            src_ref=y_send.at[k], dst_ref=y_recv.at[k], send_sem=y_ss.at[k],
            recv_sem=y_rs.at[k], device_id=hpar, device_id_type=MESH,
        )

    def piece(k, hh, xx, cols):
        r0 = pl.multiple_of((hh * 4 + xx) * 8, 8)
        return jnp.concatenate(
            [part[k, 0, pl.ds(r0, 8), cols], part[k, 1, pl.ds(r0, 8), cols]], axis=0
        )

    halves = (slice(0, HW), slice(HW, CW))
    ahead = ((x + 1) % 4, (x + 3) % 4)
    far = (x + 2) % 4

    for k in range(NCOL):
        for half in range(2):
            rows = slice(half * (D // 2) + k * CW, half * (D // 2) + (k + 1) * CW)
            part[k, half] = dot(dk, kw[rows, :], NT) + dot(dv, vw[rows, :], NT)
        for side in range(2):
            for hh in range(2):
                x1_send[k, side, 0, hh] = piece(k, hh, far, halves[side]).astype(BF)
                x1_send[k, side, 1, hh] = piece(k, hh, ahead[side], halves[1 - side]).astype(BF)
            x_copy(x1_send, x1_recv, x1_ss, x1_rs, k, side).start()
    for k in range(NCOL):
        for side in range(2):
            x_copy(x1_send, x1_recv, x1_ss, x1_rs, k, side).wait_recv()
            for hh in range(2):
                mine = piece(k, hh, ahead[side], halves[side])
                x2_send[k, side, hh] = (mine + x1_recv[k, side, 0, hh].astype(F32)).astype(BF)
            x_copy(x2_send, x2_recv, x2_ss, x2_rs, k, side).start()
    for k in range(NCOL):
        for side in range(2):
            x_copy(x2_send, x2_recv, x2_ss, x2_rs, k, side).wait_recv()
        for half in range(2):
            def gathered(hh):
                return (
                    piece(k, hh, x, halves[half])
                    + x2_recv[k, half, hh].astype(F32)
                    + x1_recv[k, 1 - half, 1, hh].astype(F32)
                )

            y_keep[k, :, halves[half]] = gathered(yh)
            y_send[k, :, halves[half]] = gathered(1 - yh).astype(BF)
        y_copy(k).start()
    for k in range(NCOL):
        y_copy(k).wait_recv()
        full = y_keep[k] + y_recv[k].astype(F32)
        o_in[:, k * CW : (k + 1) * CW] = full[0:8].astype(BF)
        o_in[:, D // 2 + k * CW : D // 2 + (k + 1) * CW] = full[8:16].astype(BF)
    for k in range(NCOL):
        for side in range(2):
            x_copy(x1_send, x1_recv, x1_ss, x1_rs, k, side).wait_send()
            x_copy(x2_send, x2_recv, x2_ss, x2_rs, k, side).wait_send()
        y_copy(k).wait_send()


def body(*args):
    anyspec = pl.BlockSpec(memory_space=pl.ANY)
    vspec = pl.BlockSpec(memory_space=pltpu.VMEM)
    sspec = pl.BlockSpec(memory_space=pltpu.SMEM)
    shape = jax.ShapeDtypeStruct
    dma = pltpu.SemaphoreType.DMA
    rows = HEADS * (SR + PR)
    return pl.pallas_call(
        body_kernel,
        in_specs=[anyspec] * 8 + [sspec] + [anyspec] * 2,
        out_specs=[vspec] * 7,
        out_shape=[
            shape((PR, HEADS * HD), BF),
            shape((PR, HD), BF),
            shape((PR, HD), BF),
            shape((1, SR, HEADS * HD), BF),
            shape((1, SR, HD), BF),
            shape((1, SR, HD), BF),
            shape((8, D), BF),
        ],
        scratch_shapes=[
            pltpu.VMEM((ROLL + 4, 2, PR, HD), BF),
            pltpu.VMEM((HD, KEYS + SR), BF),
            pltpu.VMEM((rows, HD), BF),
            pltpu.VMEM((rows, HD), BF),
            pltpu.VMEM((KEYS + SR, rows), BF),
            pltpu.VMEM((KEYS + SR, rows), BF),
            pltpu.VMEM((KEYS + SR, SR), F32),
            pltpu.VMEM((KEYS + SR, SR), F32),
            pltpu.VMEM((D, HD), BF),
            pltpu.VMEM((D, HD), BF),
            pltpu.VMEM((8, 2, PR, 2 * HD), BF),
            pltpu.VMEM((8, 2, PR, 2 * HD), F32),
            pltpu.VMEM((8, 2, PR, 2 * HD), BF),
            pltpu.VMEM((8, PR, 2 * HD), BF),
            pltpu.VMEM((8, PR, 2 * HD), F32),
            pltpu.VMEM((8, PR, 2 * HD), BF),
            pltpu.VMEM((8, PR, 2 * HD), BF),
            pltpu.VMEM((8, PR, 2 * HD), BF),
            pltpu.VMEM((NCOL, 2, 64, CW), F32),
            pltpu.VMEM((NCOL, 2, 2, 2, 16, HW), BF),
            pltpu.VMEM((NCOL, 2, 2, 2, 16, HW), BF),
            pltpu.VMEM((NCOL, 2, 2, 16, HW), BF),
            pltpu.VMEM((NCOL, 2, 2, 16, HW), BF),
            pltpu.VMEM((NCOL, 16, CW), F32),
            pltpu.VMEM((NCOL, 16, CW), BF),
            pltpu.VMEM((NCOL, 16, CW), BF),
            dma((44,)),
            dma((31,)),
            dma((32,)),
            dma((8,)),
            dma((8,)),
            dma((8,)),
            dma((8,)),
            dma((8,)),
            dma((8,)),
            dma((NCOL, 2)),
            dma((NCOL, 2)),
            dma((NCOL, 2)),
            dma((NCOL, 2)),
            dma((NCOL,)),
            dma((NCOL,)),
        ],
        compiler_params=pltpu.CompilerParams(
            collective_id=0, has_side_effects=True, vmem_limit_bytes=60 * 1024 * 1024
        ),
    )(*args)


def solution(mesh):
    placed = (
        P("roll", "kv"),
        P("roll", "kv"),
        P("roll", "kv"),
        P("roll", "kv"),
        P("roll", None, "kv"),
        P("roll", None, "kv"),
        P("roll", None, "kv"),
        P("roll", None, "kv"),
        P("roll"),
        P(None, "kv"),
        P(None, "kv"),
    )
    return jax.shard_map(
        lambda *args: tuple(body(*args)),
        mesh=mesh,
        in_specs=placed,
        out_specs=(
            P("roll", "kv"),
            P("roll", "kv"),
            P("roll", "kv"),
            P("roll", None, "kv"),
            P("roll", None, "kv"),
            P("roll", None, "kv"),
            P(("roll", "kv"), None),
        ),
        check_vma=False,
    )
```

```python
import functools

import jax
import jax.numpy as jnp
from jax import lax
from jax.experimental import pallas as pl
from jax.experimental.pallas import tpu as pltpu
from jax.sharding import PartitionSpec as P

F32 = jnp.float32
BF = jnp.bfloat16
HD = 128
HEADS = 8
PR = 64
SR = 256
ROLL = 32
KEYS = 2048
CK = 256
SCALE = HD**-0.5
ALPHA = SCALE * 1.4426950408889634
NEG = -1e30
NT = (((1,), (1,)), ((), ()))
NN = (((1,), (0,)), ((), ()))
MESH = pl.DeviceIdType.MESH
D = 8192
NCOL = 4
CW = D // 2 // NCOL
HW = CW // 2


def dot(a, b, dims):
    return lax.dot_general(a, b, dims, preferred_element_type=F32)


def fold(x, op):
    return op(x.reshape(x.shape[0] // 8, 8, x.shape[1]), axis=0)


def body_kernel(
    pq, pk, pv, pdo, sq, sk, sv, sdo, ln, kw_hbm, vw_hbm,
    o_pdq, o_pdk, o_pdv, o_sdq, o_sdk, o_sdv, o_in,
    kv, kt, q, do, ex, dsc, dp_s, s_s, kw, vw,
    a_send, a_keep, a_recv, b_send, b_keep, b_recv, c_send, c_recv,
    part, x1_send, x1_recv, x2_send, x2_recv, y_keep, y_send, y_recv,
    loc, ag_s, ag_r, a_ss, a_rs, b_ss, b_rs, c_ss, c_rs,
    x1_ss, x1_rs, x2_ss, x2_rs, y_ss, y_rs,
):
    roll = lax.axis_index("roll")
    grp = lax.axis_index("kv")
    z = roll // 4
    y = (roll // 2) % 2
    c = roll % 2
    yh = grp // 4
    x = grp % 4

    def rdev(zz, yy, cc):
        return (zz * 4 + yy * 2 + cc, grp)

    def kdev(hh, xx):
        return (roll, hh * 4 + xx)

    sib = rdev(z, y, 1 - c)
    ypar = rdev(z, 1 - y, c)
    xp = kdev(yh, (x + 1) % 4)
    xm = kdev(yh, (x + 3) % 4)
    hpar = kdev(1 - yh, x)

    copies = []

    def local(src, dst):
        cp = pltpu.make_async_copy(src, dst, loc.at[len(copies)])
        cp.start()
        copies.append(cp)

    local(pk, kv.at[roll, 0])
    local(pv, kv.at[roll, 1])
    for h in range(HEADS):
        cols = slice(h * HD, (h + 1) * HD)
        local(sq.at[0, :, cols], q.at[h * SR : (h + 1) * SR, :])
        local(sdo.at[0, :, cols], do.at[h * SR : (h + 1) * SR, :])
        base = HEADS * SR + h * PR
        local(pq.at[:, cols], q.at[base : base + PR, :])
        local(pdo.at[:, cols], do.at[base : base + PR, :])
    for i in range(4):
        local(sk.at[0, i * PR : (i + 1) * PR, :], kv.at[ROLL + i, 0])
        local(sv.at[0, i * PR : (i + 1) * PR, :], kv.at[ROLL + i, 1])
    local(kw_hbm, kw)
    local(vw_hbm, vw)

    barrier = pltpu.get_barrier_semaphore()
    peers = [rdev((z + d) % 8, y, c) for d in range(1, 8)] + [sib, ypar, xp, xm, hpar]
    for peer in peers:
        pl.semaphore_signal(barrier, inc=1, device_id=peer, device_id_type=MESH)
    pl.semaphore_wait(barrier, len(peers))

    def gather_copy(block, peer, slot):
        return pltpu.make_async_remote_copy(
            src_ref=kv.at[block], dst_ref=kv.at[block],
            send_sem=ag_s.at[slot], recv_sem=ag_r.at[block],
            device_id=peer, device_id_type=MESH,
        )

    sends = []

    def push(block, peer):
        cp = gather_copy(block, peer, len(sends))
        cp.start()
        sends.append(cp)

    copies[0].wait()
    copies[1].wait()
    order = (1, 7, 2, 6, 3, 5, 4)
    for d in order:
        push(roll, rdev((z + d) % 8, y, c))
    push(roll, ypar)
    push(roll, sib)
    for d in order:
        src = ((z + 8 - d) % 8) * 4 + y * 2 + c
        gather_copy(src, sib, 0).wait_recv()
        push(src, ypar)
        push(src, sib)
    for d in (0,) + order:
        src = ((z + 8 - d) % 8) * 4 + (1 - y) * 2 + c
        gather_copy(src, sib, 0).wait_recv()
        push(src, sib)
    for cp in copies[2:-2]:
        cp.wait()
    for d in (0,) + order:
        for yy in range(2):
            src = ((z + 8 - d) % 8) * 4 + yy * 2 + 1 - c
            gather_copy(src, sib, 0).wait_recv()
    for cp in sends:
        cp.wait_send()

    def keys(i):
        return kv[4 * i : 4 * i + 4, 0].reshape(CK, HD)

    def values(i):
        return kv[4 * i : 4 * i + 4, 1].reshape(CK, HD)

    n_live = ln[0]
    for i in range(9):
        kt[:, i * CK : (i + 1) * CK] = keys(i).T
    live = lax.broadcasted_iota(jnp.int32, (SR, HD), 0) < n_live
    for h in range(HEADS):
        rows = slice(h * SR, (h + 1) * SR)
        do[rows, :] = jnp.where(live, do[rows, :], jnp.zeros((), BF))
    kpos = lax.broadcasted_iota(jnp.int32, (CK, SR), 0)
    qpos = lax.broadcasted_iota(jnp.int32, (CK, SR), 1)

    def own_mask(i, s):
        if i < 8:
            return s
        return jnp.where((kpos <= qpos) & (kpos < n_live), s, NEG)

    def causal_mask(i, s):
        return jnp.where(kpos + i * CK <= roll * PR + (qpos & (PR - 1)), s, NEG)

    def tile(t, slot, chunks, mask, finish):
        r0 = pl.multiple_of(t * SR, SR)
        cols = pl.ds(r0, SR)
        qt = q[cols, :]
        dt = do[cols, :]
        top = jnp.full((8, SR), NEG, F32)
        for i in range(chunks):
            s = mask(i, dot(keys(i), qt, NT))
            s_s[slot, i * CK : (i + 1) * CK, :] = s
            top = jnp.maximum(top, fold(s, jnp.max))
        yield
        top = jnp.max(top, axis=0, keepdims=True) * ALPHA
        total = jnp.zeros((8, SR), F32)
        delta = jnp.zeros((8, SR), F32)
        for i in range(chunks):
            rows = slice(i * CK, (i + 1) * CK)
            e = jnp.exp2(s_s[slot, rows, :] * ALPHA - top)
            dp = dot(values(i), dt, NT)
            total = total + fold(e, jnp.sum)
            delta = delta + fold(e * dp, jnp.sum)
            s_s[slot, rows, :] = e
            dp_s[slot, rows, :] = dp
        inv = 1.0 / jnp.sum(total, axis=0, keepdims=True)
        delta = jnp.sum(delta, axis=0, keepdims=True) * inv
        yield
        acc = jnp.zeros((HD, SR), F32)
        for i in range(chunks):
            rows = slice(i * CK, (i + 1) * CK)
            p = s_s[slot, rows, :] * inv
            ds = (p * (dp_s[slot, rows, :] - delta)).astype(BF)
            ex[rows, cols] = p.astype(BF)
            dsc[rows, cols] = ds
            acc = acc + dot(kt[:, rows], ds, NN)
        finish(t, (acc * SCALE).T.astype(BF))
        yield

    def pair(t, chunks, mask, finish):
        tiles = [tile(2 * t + slot, slot, chunks, mask, finish) for slot in range(2)]
        for _ in range(3):
            for one in tiles:
                next(one)

    def roll_out(t, dq):
        o_sdq[0, :, pl.ds(pl.multiple_of(t * HD, HD), HD)] = dq

    def roll_pair(t, carry):
        pair(t, 9, own_mask, roll_out)
        return carry

    lax.fori_loop(0, HEADS // 2, roll_pair, 0)

    def prompt_out(t, dq):
        for h in range(4):
            col = pl.multiple_of(((t - HEADS) * 4 + h) * HD, HD)
            o_pdq[:, pl.ds(col, HD)] = dq[h * PR : (h + 1) * PR, :]

    def prompt_pair(t, carry):
        pair(t, 8, causal_mask, prompt_out)
        return carry

    lax.fori_loop(HEADS // 2, HEADS // 2 + 1, prompt_pair, 0)

    own = slice(KEYS, KEYS + SR)
    live_rows = HEADS * SR

    def zoff(i):
        return (z + 4 + (1 - 2 * (i % 2)) * ((i + 1) // 2)) % 8

    def a_copy(i):
        return pltpu.make_async_remote_copy(
            src_ref=a_send.at[i], dst_ref=a_recv.at[i], send_sem=a_ss.at[i],
            recv_sem=a_rs.at[i], device_id=sib, device_id_type=MESH,
        )

    def b_copy(i):
        return pltpu.make_async_remote_copy(
            src_ref=b_send.at[i], dst_ref=b_recv.at[i], send_sem=b_ss.at[i],
            recv_sem=b_rs.at[i], device_id=ypar, device_id_type=MESH,
        )

    def c_copy(i, slot, zz):
        return pltpu.make_async_remote_copy(
            src_ref=c_send.at[i], dst_ref=c_recv.at[slot], send_sem=c_ss.at[i],
            recv_sem=c_rs.at[slot], device_id=rdev(zz, y, c), device_id_type=MESH,
        )

    first_core = c == 0
    first_y = y == 0

    def compute(i):
        k0 = pl.multiple_of(zoff(i) * CK, CK)
        dk = dot(dsc[pl.ds(k0, CK), :], q[...], NN)
        dv = dot(ex[pl.ds(k0, CK), :], do[...], NN)
        for yy in range(2):
            lo = slice(yy * 2 * PR, yy * 2 * PR + PR)
            hi = slice(yy * 2 * PR + PR, yy * 2 * PR + 2 * PR)
            for part_, g in ((0, dk), (1, dv)):
                col = slice(part_ * HD, (part_ + 1) * HD)
                a_keep[i, yy, :, col] = jnp.where(first_core, g[lo], g[hi])
                a_send[i, yy, :, col] = jnp.where(first_core, g[hi], g[lo]).astype(BF)
        a_copy(i).start()

    def after_a(i):
        a_copy(i).wait_recv()
        s0 = a_keep[i, 0] + a_recv[i, 0].astype(F32)
        s1 = a_keep[i, 1] + a_recv[i, 1].astype(F32)
        b_keep[i] = jnp.where(first_y, s0, s1)
        b_send[i] = jnp.where(first_y, s1, s0).astype(BF)
        b_copy(i).start()

    def after_b(i):
        b_copy(i).wait_recv()
        return b_keep[i] + b_recv[i].astype(F32)

    def send_c(i):
        c_send[i] = after_b(i).astype(BF)
        c_copy(i, z, zoff(i)).start()

    def grads(i, carry):
        compute(i)

        @pl.when(i >= 1)
        def _():
            after_a(i - 1)

        @pl.when(i >= 2)
        def _():
            send_c(i - 2)

        return carry

    lax.fori_loop(0, 8, grads, 0)
    after_a(7)
    send_c(6)
    o_sdv[0] = dot(ex[own, 0:live_rows], do[0:live_rows, :], NN).astype(BF)
    o_sdk[0] = (dot(dsc[own, 0:live_rows], q[0:live_rows, :], NN) * SCALE).astype(BF)
    summed = after_b(7)
    for d in (1, 7, 2, 6, 3, 5, 4):
        slot = (z + d) % 8
        c_copy(0, slot, slot).wait_recv()
        summed = summed + c_recv[slot].astype(F32)
    dk = (summed[:, :HD] * SCALE).astype(BF)
    dv = summed[:, HD:].astype(BF)
    o_pdk[...] = dk
    o_pdv[...] = dv
    for i in range(8):
        a_copy(i).wait_send()
        b_copy(i).wait_send()
    for i in range(7):
        c_copy(i, z, zoff(i)).wait_send()
    copies[-2].wait()
    copies[-1].wait()

    def x_copy(send, recv, ss, rs, k, side):
        return pltpu.make_async_remote_copy(
            src_ref=send.at[k, side], dst_ref=recv.at[k, side], send_sem=ss.at[k, side],
            recv_sem=rs.at[k, side], device_id=(xp, xm)[side], device_id_type=MESH,
        )

    def y_copy(k):
        return pltpu.make_async_remote_copy(
            src_ref=y_send.at[k], dst_ref=y_recv.at[k], send_sem=y_ss.at[k],
            recv_sem=y_rs.at[k], device_id=hpar, device_id_type=MESH,
        )

    def piece(k, hh, xx, cols):
        r0 = pl.multiple_of((hh * 4 + xx) * 8, 8)
        return jnp.concatenate(
            [part[k, 0, pl.ds(r0, 8), cols], part[k, 1, pl.ds(r0, 8), cols]], axis=0
        )

    halves = (slice(0, HW), slice(HW, CW))
    ahead = ((x + 1) % 4, (x + 3) % 4)
    far = (x + 2) % 4

    for k in range(NCOL):
        for half in range(2):
            rows = slice(half * (D // 2) + k * CW, half * (D // 2) + (k + 1) * CW)
            part[k, half] = dot(dk, kw[rows, :], NT) + dot(dv, vw[rows, :], NT)
        for side in range(2):
            for hh in range(2):
                x1_send[k, side, 0, hh] = piece(k, hh, far, halves[side]).astype(BF)
                x1_send[k, side, 1, hh] = piece(k, hh, ahead[side], halves[1 - side]).astype(BF)
            x_copy(x1_send, x1_recv, x1_ss, x1_rs, k, side).start()
    for k in range(NCOL):
        for side in range(2):
            x_copy(x1_send, x1_recv, x1_ss, x1_rs, k, side).wait_recv()
            for hh in range(2):
                mine = piece(k, hh, ahead[side], halves[side])
                x2_send[k, side, hh] = (mine + x1_recv[k, side, 0, hh].astype(F32)).astype(BF)
            x_copy(x2_send, x2_recv, x2_ss, x2_rs, k, side).start()
    for k in range(NCOL):
        for side in range(2):
            x_copy(x2_send, x2_recv, x2_ss, x2_rs, k, side).wait_recv()
        for half in range(2):
            def gathered(hh):
                return (
                    piece(k, hh, x, halves[half])
                    + x2_recv[k, half, hh].astype(F32)
                    + x1_recv[k, 1 - half, 1, hh].astype(F32)
                )

            y_keep[k, :, halves[half]] = gathered(yh)
            y_send[k, :, halves[half]] = gathered(1 - yh).astype(BF)
        y_copy(k).start()
    for k in range(NCOL):
        y_copy(k).wait_recv()
        full = y_keep[k] + y_recv[k].astype(F32)
        o_in[:, k * CW : (k + 1) * CW] = full[0:8].astype(BF)
        o_in[:, D // 2 + k * CW : D // 2 + (k + 1) * CW] = full[8:16].astype(BF)
    for k in range(NCOL):
        for side in range(2):
            x_copy(x1_send, x1_recv, x1_ss, x1_rs, k, side).wait_send()
            x_copy(x2_send, x2_recv, x2_ss, x2_rs, k, side).wait_send()
        y_copy(k).wait_send()


def hand_on_kernel(*refs):
    count = len(refs) // 2
    copies = []
    for i in range(count):
        cp = pltpu.make_async_copy(refs[i], refs[count + i], refs[-1].at[i])
        cp.start()
        copies.append(cp)
    for cp in copies:
        cp.wait()


def hand_on(arrays):
    spec = pl.BlockSpec(memory_space=pl.ANY)
    vspec = pl.BlockSpec(memory_space=pltpu.VMEM)
    return pl.pallas_call(
        hand_on_kernel,
        in_specs=[vspec] * len(arrays),
        out_specs=[spec] * len(arrays),
        out_shape=[jax.ShapeDtypeStruct(a.shape, a.dtype) for a in arrays],
        scratch_shapes=[pltpu.SemaphoreType.DMA((len(arrays),))],
    )(*arrays)


def body(*args):
    anyspec = pl.BlockSpec(memory_space=pl.ANY)
    vspec = pl.BlockSpec(memory_space=pltpu.VMEM)
    sspec = pl.BlockSpec(memory_space=pltpu.SMEM)
    shape = jax.ShapeDtypeStruct
    dma = pltpu.SemaphoreType.DMA
    rows = HEADS * (SR + PR)
    return pl.pallas_call(
        body_kernel,
        in_specs=[anyspec] * 8 + [sspec] + [anyspec] * 2,
        out_specs=[vspec] * 7,
        out_shape=[
            shape((PR, HEADS * HD), BF),
            shape((PR, HD), BF),
            shape((PR, HD), BF),
            shape((1, SR, HEADS * HD), BF),
            shape((1, SR, HD), BF),
            shape((1, SR, HD), BF),
            shape((8, D), BF),
        ],
        scratch_shapes=[
            pltpu.VMEM((ROLL + 4, 2, PR, HD), BF),
            pltpu.VMEM((HD, KEYS + SR), BF),
            pltpu.VMEM((rows, HD), BF),
            pltpu.VMEM((rows, HD), BF),
            pltpu.VMEM((KEYS + SR, rows), BF),
            pltpu.VMEM((KEYS + SR, rows), BF),
            pltpu.VMEM((2, KEYS + SR, SR), F32),
            pltpu.VMEM((2, KEYS + SR, SR), F32),
            pltpu.VMEM((D, HD), BF),
            pltpu.VMEM((D, HD), BF),
            pltpu.VMEM((8, 2, PR, 2 * HD), BF),
            pltpu.VMEM((8, 2, PR, 2 * HD), F32),
            pltpu.VMEM((8, 2, PR, 2 * HD), BF),
            pltpu.VMEM((8, PR, 2 * HD), BF),
            pltpu.VMEM((8, PR, 2 * HD), F32),
            pltpu.VMEM((8, PR, 2 * HD), BF),
            pltpu.VMEM((8, PR, 2 * HD), BF),
            pltpu.VMEM((8, PR, 2 * HD), BF),
            pltpu.VMEM((NCOL, 2, 64, CW), F32),
            pltpu.VMEM((NCOL, 2, 2, 2, 16, HW), BF),
            pltpu.VMEM((NCOL, 2, 2, 2, 16, HW), BF),
            pltpu.VMEM((NCOL, 2, 2, 16, HW), BF),
            pltpu.VMEM((NCOL, 2, 2, 16, HW), BF),
            pltpu.VMEM((NCOL, 16, CW), F32),
            pltpu.VMEM((NCOL, 16, CW), BF),
            pltpu.VMEM((NCOL, 16, CW), BF),
            dma((44,)),
            dma((31,)),
            dma((32,)),
            dma((8,)),
            dma((8,)),
            dma((8,)),
            dma((8,)),
            dma((8,)),
            dma((8,)),
            dma((NCOL, 2)),
            dma((NCOL, 2)),
            dma((NCOL, 2)),
            dma((NCOL, 2)),
            dma((NCOL,)),
            dma((NCOL,)),
        ],
        compiler_params=pltpu.CompilerParams(
            collective_id=0, has_side_effects=True, vmem_limit_bytes=60 * 1024 * 1024
        ),
    )(*args)


def solution(mesh):
    placed = (
        P("roll", "kv"),
        P("roll", "kv"),
        P("roll", "kv"),
        P("roll", "kv"),
        P("roll", None, "kv"),
        P("roll", None, "kv"),
        P("roll", None, "kv"),
        P("roll", None, "kv"),
        P("roll"),
        P(None, "kv"),
        P(None, "kv"),
    )
    return jax.shard_map(
        lambda *args: tuple(hand_on(body(*args))),
        mesh=mesh,
        in_specs=placed,
        out_specs=(
            P("roll", "kv"),
            P("roll", "kv"),
            P("roll", "kv"),
            P("roll", None, "kv"),
            P("roll", None, "kv"),
            P("roll", None, "kv"),
            P(("roll", "kv"), None),
        ),
        check_vma=False,
    )
```

```python
import functools

import jax
import jax.numpy as jnp
from jax import lax
from jax.experimental import pallas as pl
from jax.experimental.pallas import tpu as pltpu
from jax.sharding import PartitionSpec as P

F32 = jnp.float32
BF = jnp.bfloat16
HD = 128
HEADS = 8
PR = 64
HR = PR // 2
SR = 256
ROLL = 32
KEYS = 2048
CK = 256
SCALE = HD**-0.5
ALPHA = SCALE * 1.4426950408889634
NEG = -1e30
NT = (((1,), (1,)), ((), ()))
NN = (((1,), (0,)), ((), ()))
MESH = pl.DeviceIdType.MESH
D = 8192
NCOL = 4
CW = D // 2 // NCOL
HW = CW // 2
LAG_A = 2
LAG_B = 4


def dot(a, b, dims):
    return lax.dot_general(a, b, dims, preferred_element_type=F32)


def fold(x, op):
    return op(x.reshape(x.shape[0] // 8, 8, x.shape[1]), axis=0)


def body_kernel(
    pq, pk, pv, pdo, sq, sk, sv, sdo, ln, kw_hbm, vw_hbm,
    o_pdq, o_pdk, o_pdv, o_sdq, o_sdk, o_sdv, o_in,
    kv, kt, q, do, ex, dsc, dp_s, s_s, kw, vw,
    a_send, a_keep, a_recv, b_send, b_keep, b_recv, c_send, c_recv, own_keep,
    part, x1_send, x1_recv, x2_send, x2_recv, y_keep, y_send, y_recv,
    loc, ag_s, ag_r, a_ss, a_rs, b_ss, b_rs, c_ss, c_rs,
    x1_ss, x1_rs, x2_ss, x2_rs, y_ss, y_rs,
):
    roll = lax.axis_index("roll")
    grp = lax.axis_index("kv")
    z = roll // 4
    y = (roll // 2) % 2
    c = roll % 2
    yh = grp // 4
    x = grp % 4

    def rdev(zz, yy, cc):
        return (zz * 4 + yy * 2 + cc, grp)

    def kdev(hh, xx):
        return (roll, hh * 4 + xx)

    sib = rdev(z, y, 1 - c)
    ypar = rdev(z, 1 - y, c)
    xp = kdev(yh, (x + 1) % 4)
    xm = kdev(yh, (x + 3) % 4)
    hpar = kdev(1 - yh, x)

    copies = []

    def local(src, dst):
        cp = pltpu.make_async_copy(src, dst, loc.at[len(copies)])
        cp.start()
        copies.append(cp)

    local(pk, kv.at[roll, 0])
    local(pv, kv.at[roll, 1])
    for h in range(HEADS):
        cols = slice(h * HD, (h + 1) * HD)
        local(sq.at[0, :, cols], q.at[h * SR : (h + 1) * SR, :])
        local(sdo.at[0, :, cols], do.at[h * SR : (h + 1) * SR, :])
        base = HEADS * SR + h * PR
        local(pq.at[:, cols], q.at[base : base + PR, :])
        local(pdo.at[:, cols], do.at[base : base + PR, :])
    for i in range(4):
        local(sk.at[0, i * PR : (i + 1) * PR, :], kv.at[ROLL + i, 0])
        local(sv.at[0, i * PR : (i + 1) * PR, :], kv.at[ROLL + i, 1])
    local(kw_hbm, kw)
    local(vw_hbm, vw)

    barrier = pltpu.get_barrier_semaphore()
    peers = [rdev((z + d) % 8, y, c) for d in range(1, 8)] + [sib, ypar, xp, xm, hpar]
    for peer in peers:
        pl.semaphore_signal(barrier, inc=1, device_id=peer, device_id_type=MESH)
    pl.semaphore_wait(barrier, len(peers))

    def gather_copy(block, peer, slot):
        return pltpu.make_async_remote_copy(
            src_ref=kv.at[block], dst_ref=kv.at[block],
            send_sem=ag_s.at[slot], recv_sem=ag_r.at[block],
            device_id=peer, device_id_type=MESH,
        )

    sends = []

    def push(block, peer):
        cp = gather_copy(block, peer, len(sends))
        cp.start()
        sends.append(cp)

    copies[0].wait()
    copies[1].wait()
    order = (1, 7, 2, 6, 3, 5, 4)
    for d in order:
        push(roll, rdev((z + d) % 8, y, c))
    push(roll, ypar)
    push(roll, sib)
    for d in order:
        src = ((z + 8 - d) % 8) * 4 + y * 2 + c
        gather_copy(src, sib, 0).wait_recv()
        push(src, ypar)
        push(src, sib)
    for d in (0,) + order:
        src = ((z + 8 - d) % 8) * 4 + (1 - y) * 2 + c
        gather_copy(src, sib, 0).wait_recv()
        push(src, sib)
    for cp in copies[2:-2]:
        cp.wait()
    for d in (0,) + order:
        for yy in range(2):
            src = ((z + 8 - d) % 8) * 4 + yy * 2 + 1 - c
            gather_copy(src, sib, 0).wait_recv()
    for cp in sends:
        cp.wait_send()

    def keys(i):
        return kv[4 * i : 4 * i + 4, 0].reshape(CK, HD)

    def values(i):
        return kv[4 * i : 4 * i + 4, 1].reshape(CK, HD)

    n_live = ln[0]
    for i in range(9):
        kt[:, i * CK : (i + 1) * CK] = keys(i).T
    live = lax.broadcasted_iota(jnp.int32, (SR, HD), 0) < n_live
    for h in range(HEADS):
        rows = slice(h * SR, (h + 1) * SR)
        do[rows, :] = jnp.where(live, do[rows, :], jnp.zeros((), BF))
    kpos = lax.broadcasted_iota(jnp.int32, (CK, SR), 0)
    qpos = lax.broadcasted_iota(jnp.int32, (CK, SR), 1)

    def own_mask(i, s):
        if i < 8:
            return s
        return jnp.where((kpos <= qpos) & (kpos < n_live), s, NEG)

    def causal_mask(i, s):
        return jnp.where(kpos + i * CK <= roll * PR + (qpos & (PR - 1)), s, NEG)

    def tile(t, slot, chunks, mask, finish):
        r0 = pl.multiple_of(t * SR, SR)
        cols = pl.ds(r0, SR)
        qt = q[cols, :]
        dt = do[cols, :]
        top = jnp.full((8, SR), NEG, F32)
        for i in range(chunks):
            s = mask(i, dot(keys(i), qt, NT))
            s_s[slot, i * CK : (i + 1) * CK, :] = s
            top = jnp.maximum(top, fold(s, jnp.max))
        yield
        top = jnp.max(top, axis=0, keepdims=True) * ALPHA
        total = jnp.zeros((8, SR), F32)
        delta = jnp.zeros((8, SR), F32)
        for i in range(chunks):
            rows = slice(i * CK, (i + 1) * CK)
            e = jnp.exp2(s_s[slot, rows, :] * ALPHA - top)
            dp = dot(values(i), dt, NT)
            total = total + fold(e, jnp.sum)
            delta = delta + fold(e * dp, jnp.sum)
            s_s[slot, rows, :] = e
            dp_s[slot, rows, :] = dp
        inv = 1.0 / jnp.sum(total, axis=0, keepdims=True)
        delta = jnp.sum(delta, axis=0, keepdims=True) * inv
        yield
        acc = jnp.zeros((HD, SR), F32)
        for i in range(chunks):
            rows = slice(i * CK, (i + 1) * CK)
            p = s_s[slot, rows, :] * inv
            ds = (p * (dp_s[slot, rows, :] - delta)).astype(BF)
            ex[rows, cols] = p.astype(BF)
            dsc[rows, cols] = ds
            acc = acc + dot(kt[:, rows], ds, NN)
        finish(t, (acc * SCALE).T.astype(BF))
        yield

    def pair(t, chunks, mask, finish):
        tiles = [tile(2 * t + slot, slot, chunks, mask, finish) for slot in range(2)]
        for _ in range(3):
            for one in tiles:
                next(one)

    def roll_out(t, dq):
        o_sdq[0, :, pl.ds(pl.multiple_of(t * HD, HD), HD)] = dq

    def roll_pair(t, carry):
        pair(t, 9, own_mask, roll_out)
        return carry

    lax.fori_loop(0, HEADS // 2, roll_pair, 0)

    def prompt_out(t, dq):
        for h in range(4):
            col = pl.multiple_of(((t - HEADS) * 4 + h) * HD, HD)
            o_pdq[:, pl.ds(col, HD)] = dq[h * PR : (h + 1) * PR, :]

    def prompt_pair(t, carry):
        pair(t, 8, causal_mask, prompt_out)
        return carry

    lax.fori_loop(HEADS // 2, HEADS // 2 + 1, prompt_pair, 0)

    own = slice(KEYS, KEYS + SR)
    live_rows = HEADS * SR

    def zoff(i):
        return (z + 4 + (1 - 2 * (i % 2)) * ((i + 1) // 2)) % 8

    def a_copy(i):
        return pltpu.make_async_remote_copy(
            src_ref=a_send.at[i], dst_ref=a_recv.at[i], send_sem=a_ss.at[i],
            recv_sem=a_rs.at[i], device_id=sib, device_id_type=MESH,
        )

    def b_copy(i):
        return pltpu.make_async_remote_copy(
            src_ref=b_send.at[i], dst_ref=b_recv.at[i], send_sem=b_ss.at[i],
            recv_sem=b_rs.at[i], device_id=ypar, device_id_type=MESH,
        )

    def c_copy(i, zi, zz):
        return pltpu.make_async_remote_copy(
            src_ref=c_send.at[i, zi], dst_ref=c_recv.at[i // 4, z], send_sem=c_ss.at[i, zi],
            recv_sem=c_rs.at[i // 4, z], device_id=rdev(zz, y, c), device_id_type=MESH,
        )

    def c_landed(hh, slot):
        pltpu.make_async_remote_copy(
            src_ref=c_send.at[0, 0], dst_ref=c_recv.at[hh, slot], send_sem=c_ss.at[0, 0],
            recv_sem=c_rs.at[hh, slot], device_id=sib, device_id_type=MESH,
        ).wait_recv()

    first_core = c == 0
    first_y = y == 0

    def compute(i):
        def gather(ref):
            picked = []
            for zi in range(2):
                k0 = zoff(2 * (i % 4) + zi) * CK + (i // 4) * HR
                for b in range(4):
                    picked.append(ref[pl.ds(pl.multiple_of(k0 + b * PR, HR), HR), :])
            return jnp.concatenate(picked, axis=0)

        for part_, g in ((0, dot(gather(dsc), q[...], NN)), (1, dot(gather(ex), do[...], NN))):
            col = slice(part_ * HD, (part_ + 1) * HD)
            for zi in range(2):
                for yy in range(2):
                    r0 = (zi * 4 + yy * 2) * HR
                    lo, hi = g[r0 : r0 + HR], g[r0 + HR : r0 + 2 * HR]
                    a_keep[i, zi, yy, :, col] = jnp.where(first_core, lo, hi)
                    a_send[i, zi, yy, :, col] = jnp.where(first_core, hi, lo).astype(BF)
        a_copy(i).start()

    def after_a(i):
        a_copy(i).wait_recv()
        s0 = a_keep[i, :, 0] + a_recv[i, :, 0].astype(F32)
        s1 = a_keep[i, :, 1] + a_recv[i, :, 1].astype(F32)
        b_keep[i] = jnp.where(first_y, s0, s1)
        b_send[i] = jnp.where(first_y, s1, s0).astype(BF)
        b_copy(i).start()

    def send_c(i):
        b_copy(i).wait_recv()
        both = b_keep[i] + b_recv[i].astype(F32)
        c_send[i] = both.astype(BF)
        c_copy(i, 0, zoff(2 * (i % 4))).start()

        @pl.when(i % 4 < 3)
        def _():
            c_copy(i, 1, zoff(2 * (i % 4) + 1)).start()

        @pl.when(i % 4 == 3)
        def _():
            own_keep[i // 4] = both[1]

    def grads(i, carry):
        compute(i)
        pl.when(i >= LAG_A)(lambda: after_a(i - LAG_A))
        pl.when(i >= LAG_B)(lambda: send_c(i - LAG_B))
        return carry

    lax.fori_loop(0, 8, grads, 0)

    def rest_a(i, carry):
        after_a(i)
        return carry

    def rest_c(i, carry):
        send_c(i)
        return carry

    lax.fori_loop(8 - LAG_A, 8, rest_a, 0)
    lax.fori_loop(8 - LAG_B, 6, rest_c, 0)
    o_sdv[0] = dot(ex[own, 0:live_rows], do[0:live_rows, :], NN).astype(BF)
    o_sdk[0] = (dot(dsc[own, 0:live_rows], q[0:live_rows, :], NN) * SCALE).astype(BF)
    lax.fori_loop(6, 8, rest_c, 0)

    copies[-2].wait()
    copies[-1].wait()

    def x_copy(send, recv, ss, rs, hh, k, side):
        return pltpu.make_async_remote_copy(
            src_ref=send.at[hh, k, side], dst_ref=recv.at[hh, k, side],
            send_sem=ss.at[hh, k, side], recv_sem=rs.at[hh, k, side],
            device_id=(xp, xm)[side], device_id_type=MESH,
        )

    def x1_copy(hh, k, side):
        return x_copy(x1_send, x1_recv, x1_ss, x1_rs, hh, k, side)

    def x2_copy(hh, k, side):
        return x_copy(x2_send, x2_recv, x2_ss, x2_rs, hh, k, side)

    def y_copy(hh, k):
        return pltpu.make_async_remote_copy(
            src_ref=y_send.at[hh, k], dst_ref=y_recv.at[k], send_sem=y_ss.at[k],
            recv_sem=y_rs.at[k], device_id=hpar, device_id_type=MESH,
        )

    def piece(hh, k, xx, cols):
        r0 = pl.multiple_of(xx * 8, 8)
        return jnp.concatenate(
            [part[hh, k, 0, pl.ds(r0, 8), cols], part[hh, k, 1, pl.ds(r0, 8), cols]], axis=0
        )

    halves = (slice(0, HW), slice(HW, CW))
    ahead = ((x + 1) % 4, (x + 3) % 4)
    far = (x + 2) % 4

    def project(hh):
        summed = own_keep[hh]
        for d in (4, 3, 5, 2, 6, 1, 7):
            slot = (z + d) % 8
            c_landed(hh, slot)
            summed = summed + c_recv[hh, slot].astype(F32)
        dk = (summed[:, :HD] * SCALE).astype(BF)
        dv = summed[:, HD:].astype(BF)
        o_pdk[hh * HR : (hh + 1) * HR, :] = dk
        o_pdv[hh * HR : (hh + 1) * HR, :] = dv
        for k in range(NCOL):
            for half in range(2):
                rows = slice(half * (D // 2) + k * CW, half * (D // 2) + (k + 1) * CW)
                part[hh, k, half] = dot(dk, kw[rows, :], NT) + dot(dv, vw[rows, :], NT)
            for side in range(2):
                x1_send[hh, k, side, 0] = piece(hh, k, far, halves[side]).astype(BF)
                x1_send[hh, k, side, 1] = piece(hh, k, ahead[side], halves[1 - side]).astype(BF)
                x1_copy(hh, k, side).start()

    def second(hh):
        for k in range(NCOL):
            for side in range(2):
                x1_copy(hh, k, side).wait_recv()
                mine = piece(hh, k, ahead[side], halves[side])
                x2_send[hh, k, side] = (mine + x1_recv[hh, k, side, 0].astype(F32)).astype(BF)
                x2_copy(hh, k, side).start()

    def third(hh):
        for k in range(NCOL):
            for side in range(2):
                x2_copy(hh, k, side).wait_recv()
            for half in range(2):
                got = (
                    piece(hh, k, x, halves[half])
                    + x2_recv[hh, k, half].astype(F32)
                    + x1_recv[hh, k, 1 - half, 1].astype(F32)
                )
                y_keep[hh, k, :, halves[half]] = got
                y_send[hh, k, :, halves[half]] = got.astype(BF)
            pl.when(yh != hh)(lambda: y_copy(hh, k).start())

    project(0)
    project(1)
    second(0)
    second(1)
    third(0)
    third(1)
    for k in range(NCOL):
        y_copy(0, k).wait_recv()
        full = y_keep[yh, k] + y_recv[k].astype(F32)
        o_in[:, k * CW : (k + 1) * CW] = full[0:8].astype(BF)
        o_in[:, D // 2 + k * CW : D // 2 + (k + 1) * CW] = full[8:16].astype(BF)
    for i in range(8):
        a_copy(i).wait_send()
        b_copy(i).wait_send()
        c_copy(i, 0, z).wait_send()
        if i % 4 < 3:
            c_copy(i, 1, z).wait_send()
    for k in range(NCOL):
        for hh in range(2):
            for side in range(2):
                x1_copy(hh, k, side).wait_send()
                x2_copy(hh, k, side).wait_send()
        y_copy(0, k).wait_send()


def hand_on_kernel(*refs):
    count = len(refs) // 2
    copies = []
    for i in range(count):
        cp = pltpu.make_async_copy(refs[i], refs[count + i], refs[-1].at[i])
        cp.start()
        copies.append(cp)
    for cp in copies:
        cp.wait()


def hand_on(arrays):
    spec = pl.BlockSpec(memory_space=pl.ANY)
    vspec = pl.BlockSpec(memory_space=pltpu.VMEM)
    return pl.pallas_call(
        hand_on_kernel,
        in_specs=[vspec] * len(arrays),
        out_specs=[spec] * len(arrays),
        out_shape=[jax.ShapeDtypeStruct(a.shape, a.dtype) for a in arrays],
        scratch_shapes=[pltpu.SemaphoreType.DMA((len(arrays),))],
    )(*arrays)


def body(*args):
    anyspec = pl.BlockSpec(memory_space=pl.ANY)
    vspec = pl.BlockSpec(memory_space=pltpu.VMEM)
    sspec = pl.BlockSpec(memory_space=pltpu.SMEM)
    shape = jax.ShapeDtypeStruct
    dma = pltpu.SemaphoreType.DMA
    rows = HEADS * (SR + PR)
    return pl.pallas_call(
        body_kernel,
        in_specs=[anyspec] * 8 + [sspec] + [anyspec] * 2,
        out_specs=[vspec] * 7,
        out_shape=[
            shape((PR, HEADS * HD), BF),
            shape((PR, HD), BF),
            shape((PR, HD), BF),
            shape((1, SR, HEADS * HD), BF),
            shape((1, SR, HD), BF),
            shape((1, SR, HD), BF),
            shape((8, D), BF),
        ],
        scratch_shapes=[
            pltpu.VMEM((ROLL + 4, 2, PR, HD), BF),
            pltpu.VMEM((HD, KEYS + SR), BF),
            pltpu.VMEM((rows, HD), BF),
            pltpu.VMEM((rows, HD), BF),
            pltpu.VMEM((KEYS + SR, rows), BF),
            pltpu.VMEM((KEYS + SR, rows), BF),
            pltpu.VMEM((2, KEYS + SR, SR), F32),
            pltpu.VMEM((2, KEYS + SR, SR), F32),
            pltpu.VMEM((D, HD), BF),
            pltpu.VMEM((D, HD), BF),
            pltpu.VMEM((8, 2, 2, HR, 2 * HD), BF),
            pltpu.VMEM((8, 2, 2, HR, 2 * HD), F32),
            pltpu.VMEM((8, 2, 2, HR, 2 * HD), BF),
            pltpu.VMEM((8, 2, HR, 2 * HD), BF),
            pltpu.VMEM((8, 2, HR, 2 * HD), F32),
            pltpu.VMEM((8, 2, HR, 2 * HD), BF),
            pltpu.VMEM((8, 2, HR, 2 * HD), BF),
            pltpu.VMEM((2, 8, HR, 2 * HD), BF),
            pltpu.VMEM((2, HR, 2 * HD), F32),
            pltpu.VMEM((2, NCOL, 2, HR, CW), F32),
            pltpu.VMEM((2, NCOL, 2, 2, 16, HW), BF),
            pltpu.VMEM((2, NCOL, 2, 2, 16, HW), BF),
            pltpu.VMEM((2, NCOL, 2, 16, HW), BF),
            pltpu.VMEM((2, NCOL, 2, 16, HW), BF),
            pltpu.VMEM((2, NCOL, 16, CW), F32),
            pltpu.VMEM((2, NCOL, 16, CW), BF),
            pltpu.VMEM((NCOL, 16, CW), BF),
            dma((44,)),
            dma((31,)),
            dma((32,)),
            dma((8,)),
            dma((8,)),
            dma((8,)),
            dma((8,)),
            dma((8, 2)),
            dma((2, 8)),
            dma((2, NCOL, 2)),
            dma((2, NCOL, 2)),
            dma((2, NCOL, 2)),
            dma((2, NCOL, 2)),
            dma((NCOL,)),
            dma((NCOL,)),
        ],
        compiler_params=pltpu.CompilerParams(
            collective_id=0, has_side_effects=True, vmem_limit_bytes=60 * 1024 * 1024
        ),
    )(*args)


def solution(mesh):
    placed = (
        P("roll", "kv"),
        P("roll", "kv"),
        P("roll", "kv"),
        P("roll", "kv"),
        P("roll", None, "kv"),
        P("roll", None, "kv"),
        P("roll", None, "kv"),
        P("roll", None, "kv"),
        P("roll"),
        P(None, "kv"),
        P(None, "kv"),
    )
    return jax.shard_map(
        lambda *args: tuple(hand_on(body(*args))),
        mesh=mesh,
        in_specs=placed,
        out_specs=(
            P("roll", "kv"),
            P("roll", "kv"),
            P("roll", "kv"),
            P("roll", None, "kv"),
            P("roll", None, "kv"),
            P("roll", None, "kv"),
            P(("roll", "kv"), None),
        ),
        check_vma=False,
    )
```

```python
import functools

import jax
import jax.numpy as jnp
from jax import lax
from jax.experimental import pallas as pl
from jax.experimental.pallas import tpu as pltpu
from jax.sharding import PartitionSpec as P

F32 = jnp.float32
BF = jnp.bfloat16
HD = 128
HEADS = 8
PR = 64
HR = PR // 2
SR = 256
ROLL = 32
KEYS = 2048
CK = 256
SCALE = HD**-0.5
ALPHA = SCALE * 1.4426950408889634
NEG = -1e30
NT = (((1,), (1,)), ((), ()))
NN = (((1,), (0,)), ((), ()))
MESH = pl.DeviceIdType.MESH
D = 8192
NCOL = 4
CW = D // 2 // NCOL
HW = CW // 2
LAG_A = 2
LAG_B = 4


def dot(a, b, dims):
    return lax.dot_general(a, b, dims, preferred_element_type=F32)


def fold(x, op):
    return op(x.reshape(x.shape[0] // 8, 8, x.shape[1]), axis=0)


def body_kernel(
    pq, pk, pv, pdo, sq, sk, sv, sdo, ln, kw_hbm, vw_hbm,
    o_pdq, o_pdk, o_pdv, o_sdq, o_sdk, o_sdv, o_in,
    kv, kt, q, do, ex, dsc, dp_s, s_s, kvw,
    a_send, a_keep, a_recv, b_send, b_keep, b_recv, c_send, c_recv, own_keep,
    part, x1_send, x1_recv, x2_send, x2_recv, y_keep, y_send, y_recv,
    loc, ag_s, ag_r, a_ss, a_rs, b_ss, b_rs, c_ss, c_rs,
    x1_ss, x1_rs, x2_ss, x2_rs, y_ss, y_rs,
):
    roll = lax.axis_index("roll")
    grp = lax.axis_index("kv")
    z = roll // 4
    y = (roll // 2) % 2
    c = roll % 2
    yh = grp // 4
    x = grp % 4

    def rdev(zz, yy, cc):
        return (zz * 4 + yy * 2 + cc, grp)

    def kdev(hh, xx):
        return (roll, hh * 4 + xx)

    sib = rdev(z, y, 1 - c)
    ypar = rdev(z, 1 - y, c)
    xp = kdev(yh, (x + 1) % 4)
    xm = kdev(yh, (x + 3) % 4)
    hpar = kdev(1 - yh, x)

    copies = []

    def local(src, dst):
        cp = pltpu.make_async_copy(src, dst, loc.at[len(copies)])
        cp.start()
        copies.append(cp)

    local(pk, kv.at[roll, 0])
    local(pv, kv.at[roll, 1])
    for h in range(HEADS):
        cols = slice(h * HD, (h + 1) * HD)
        local(sq.at[0, :, cols], q.at[h * SR : (h + 1) * SR, :])
        local(sdo.at[0, :, cols], do.at[h * SR : (h + 1) * SR, :])
        base = HEADS * SR + h * PR
        local(pq.at[:, cols], q.at[base : base + PR, :])
        local(pdo.at[:, cols], do.at[base : base + PR, :])
    for i in range(4):
        local(sk.at[0, i * PR : (i + 1) * PR, :], kv.at[ROLL + i, 0])
        local(sv.at[0, i * PR : (i + 1) * PR, :], kv.at[ROLL + i, 1])
    local(kw_hbm, kvw.at[:, 0:HD])
    local(vw_hbm, kvw.at[:, HD : 2 * HD])

    barrier = pltpu.get_barrier_semaphore()
    peers = [rdev((z + d) % 8, y, c) for d in range(1, 8)] + [sib, ypar, xp, xm, hpar]
    for peer in peers:
        pl.semaphore_signal(barrier, inc=1, device_id=peer, device_id_type=MESH)
    pl.semaphore_wait(barrier, len(peers))

    def gather_copy(block, peer, slot):
        return pltpu.make_async_remote_copy(
            src_ref=kv.at[block], dst_ref=kv.at[block],
            send_sem=ag_s.at[slot], recv_sem=ag_r.at[block],
            device_id=peer, device_id_type=MESH,
        )

    sends = []

    def push(block, peer):
        cp = gather_copy(block, peer, len(sends))
        cp.start()
        sends.append(cp)

    copies[0].wait()
    copies[1].wait()
    order = (1, 7, 2, 6, 3, 5, 4)
    for d in order:
        push(roll, rdev((z + d) % 8, y, c))
    push(roll, ypar)
    push(roll, sib)
    for d in order:
        src = ((z + 8 - d) % 8) * 4 + y * 2 + c
        gather_copy(src, sib, 0).wait_recv()
        push(src, ypar)
        push(src, sib)
    for d in (0,) + order:
        src = ((z + 8 - d) % 8) * 4 + (1 - y) * 2 + c
        gather_copy(src, sib, 0).wait_recv()
        push(src, sib)
    for cp in copies[2:-2]:
        cp.wait()
    for d in (0,) + order:
        for yy in range(2):
            src = ((z + 8 - d) % 8) * 4 + yy * 2 + 1 - c
            gather_copy(src, sib, 0).wait_recv()
    for cp in sends:
        cp.wait_send()

    def keys(i):
        return kv[4 * i : 4 * i + 4, 0].reshape(CK, HD)

    def values(i):
        return kv[4 * i : 4 * i + 4, 1].reshape(CK, HD)

    n_live = ln[0]
    live = lax.broadcasted_iota(jnp.int32, (SR, HD), 0) < n_live
    for h in range(HEADS):
        rows = slice(h * SR, (h + 1) * SR)
        do[rows, :] = jnp.where(live, do[rows, :], jnp.zeros((), BF))
    kpos = lax.broadcasted_iota(jnp.int32, (CK, SR), 0)
    qpos = lax.broadcasted_iota(jnp.int32, (CK, SR), 1)

    def own_mask(i, s):
        if i < 8:
            return s
        return jnp.where((kpos <= qpos) & (kpos < n_live), s, NEG)

    def causal_mask(i, s):
        return jnp.where(kpos + i * CK <= roll * PR + (qpos & (PR - 1)), s, NEG)

    def tile(t, slot, chunks, mask):
        r0 = pl.multiple_of(t * SR, SR)
        cols = pl.ds(r0, SR)
        qt = q[cols, :]
        dt = do[cols, :]
        top = jnp.full((8, SR), NEG, F32)
        for i in range(chunks):
            s = mask(i, dot(keys(i), qt, NT))
            s_s[slot, i * CK : (i + 1) * CK, :] = s
            top = jnp.maximum(top, fold(s, jnp.max))
        yield
        top = jnp.max(top, axis=0, keepdims=True) * ALPHA
        total = jnp.zeros((8, SR), F32)
        delta = jnp.zeros((8, SR), F32)
        for i in range(chunks):
            rows = slice(i * CK, (i + 1) * CK)
            e = jnp.exp2(s_s[slot, rows, :] * ALPHA - top)
            dp = dot(values(i), dt, NT)
            total = total + fold(e, jnp.sum)
            delta = delta + fold(e * dp, jnp.sum)
            s_s[slot, rows, :] = e
            dp_s[slot, rows, :] = dp
        inv = 1.0 / jnp.sum(total, axis=0, keepdims=True)
        delta = jnp.sum(delta, axis=0, keepdims=True) * inv
        yield
        for i in range(chunks):
            rows = slice(i * CK, (i + 1) * CK)
            p = s_s[slot, rows, :] * inv
            ds = (p * (dp_s[slot, rows, :] - delta)).astype(BF)
            ex[rows, cols] = p.astype(BF)
            dsc[rows, cols] = ds
        yield

    def pair(t, chunks, mask):
        tiles = [tile(2 * t + slot, slot, chunks, mask) for slot in range(2)]
        for _ in range(3):
            for one in tiles:
                next(one)

    def roll_pair(t, carry):
        pair(t, 9, own_mask)
        return carry

    lax.fori_loop(0, HEADS // 2, roll_pair, 0)

    def prompt_pair(t, carry):
        pair(t, 8, causal_mask)
        return carry

    lax.fori_loop(HEADS // 2, HEADS // 2 + 1, prompt_pair, 0)

    def turn_keys():
        for i in range(9):
            kt[:, i * CK : (i + 1) * CK] = keys(i).T

    def query_grad(t, rows):
        cols = pl.ds(pl.multiple_of(t * SR, SR), SR)
        return (dot(kt[:, 0:rows], dsc[0:rows, cols], NN) * SCALE).T.astype(BF)

    def roll_query(t, carry):
        o_sdq[0, :, pl.ds(pl.multiple_of(t * HD, HD), HD)] = query_grad(t, KEYS + SR)
        return carry

    def roll_queries(first, last):
        lax.fori_loop(first, last, roll_query, 0)

    def prompt_query(i):
        dq = query_grad(HEADS + i, KEYS)
        for h in range(4):
            o_pdq[:, (4 * i + h) * HD : (4 * i + h + 1) * HD] = dq[h * PR : (h + 1) * PR, :]

    own = slice(KEYS, KEYS + SR)
    live_rows = HEADS * SR

    def zoff(i):
        return (z + 4 + (1 - 2 * (i % 2)) * ((i + 1) // 2)) % 8

    def a_copy(i):
        return pltpu.make_async_remote_copy(
            src_ref=a_send.at[i], dst_ref=a_recv.at[i], send_sem=a_ss.at[i],
            recv_sem=a_rs.at[i], device_id=sib, device_id_type=MESH,
        )

    def b_copy(i):
        return pltpu.make_async_remote_copy(
            src_ref=b_send.at[i], dst_ref=b_recv.at[i], send_sem=b_ss.at[i],
            recv_sem=b_rs.at[i], device_id=ypar, device_id_type=MESH,
        )

    def c_copy(i, zi, zz):
        return pltpu.make_async_remote_copy(
            src_ref=c_send.at[i, zi], dst_ref=c_recv.at[i // 4, z], send_sem=c_ss.at[i, zi],
            recv_sem=c_rs.at[i // 4, z], device_id=rdev(zz, y, c), device_id_type=MESH,
        )

    def c_landed(hh, slot):
        pltpu.make_async_remote_copy(
            src_ref=c_send.at[0, 0], dst_ref=c_recv.at[hh, slot], send_sem=c_ss.at[0, 0],
            recv_sem=c_rs.at[hh, slot], device_id=sib, device_id_type=MESH,
        ).wait_recv()

    first_core = c == 0
    first_y = y == 0

    def compute(i):
        def gather(ref):
            picked = []
            for zi in range(2):
                k0 = zoff(2 * (i % 4) + zi) * CK + (i // 4) * HR
                for b in range(4):
                    picked.append(ref[pl.ds(pl.multiple_of(k0 + b * PR, HR), HR), :])
            return jnp.concatenate(picked, axis=0)

        for part_, g in ((0, dot(gather(dsc), q[...], NN)), (1, dot(gather(ex), do[...], NN))):
            col = slice(part_ * HD, (part_ + 1) * HD)
            for zi in range(2):
                for yy in range(2):
                    r0 = (zi * 4 + yy * 2) * HR
                    lo, hi = g[r0 : r0 + HR], g[r0 + HR : r0 + 2 * HR]
                    a_keep[i, zi, yy, :, col] = jnp.where(first_core, lo, hi)
                    a_send[i, zi, yy, :, col] = jnp.where(first_core, hi, lo).astype(BF)
        a_copy(i).start()

    def after_a(i):
        a_copy(i).wait_recv()
        s0 = a_keep[i, :, 0] + a_recv[i, :, 0].astype(F32)
        s1 = a_keep[i, :, 1] + a_recv[i, :, 1].astype(F32)
        b_keep[i] = jnp.where(first_y, s0, s1)
        b_send[i] = jnp.where(first_y, s1, s0).astype(BF)
        b_copy(i).start()

    def send_c(i):
        b_copy(i).wait_recv()
        both = b_keep[i] + b_recv[i].astype(F32)
        c_send[i] = both.astype(BF)
        c_copy(i, 0, zoff(2 * (i % 4))).start()

        @pl.when(i % 4 < 3)
        def _():
            c_copy(i, 1, zoff(2 * (i % 4) + 1)).start()

        @pl.when(i % 4 == 3)
        def _():
            own_keep[i // 4] = both[1]

    def grads(i, carry):
        compute(i)
        pl.when(i >= LAG_A)(lambda: after_a(i - LAG_A))
        pl.when(i >= LAG_B)(lambda: send_c(i - LAG_B))
        return carry

    lax.fori_loop(0, 8, grads, 0)

    def rest_a(i, carry):
        after_a(i)
        return carry

    def rest_c(i, carry):
        send_c(i)
        return carry

    lax.fori_loop(8 - LAG_A, 8, rest_a, 0)
    lax.fori_loop(8 - LAG_B, 6, rest_c, 0)
    turn_keys()
    o_sdv[0] = dot(ex[own, 0:live_rows], do[0:live_rows, :], NN).astype(BF)
    o_sdk[0] = (dot(dsc[own, 0:live_rows], q[0:live_rows, :], NN) * SCALE).astype(BF)
    lax.fori_loop(6, 8, rest_c, 0)

    copies[-2].wait()
    copies[-1].wait()

    def x_copy(send, recv, ss, rs, hh, k, side):
        return pltpu.make_async_remote_copy(
            src_ref=send.at[hh, k, side], dst_ref=recv.at[hh, k, side],
            send_sem=ss.at[hh, k, side], recv_sem=rs.at[hh, k, side],
            device_id=(xp, xm)[side], device_id_type=MESH,
        )

    def x1_copy(hh, k, side):
        return x_copy(x1_send, x1_recv, x1_ss, x1_rs, hh, k, side)

    def x2_copy(hh, k, side):
        return x_copy(x2_send, x2_recv, x2_ss, x2_rs, hh, k, side)

    def y_copy(hh, k):
        return pltpu.make_async_remote_copy(
            src_ref=y_send.at[hh, k], dst_ref=y_recv.at[k], send_sem=y_ss.at[k],
            recv_sem=y_rs.at[k], device_id=hpar, device_id_type=MESH,
        )

    def piece(hh, k, xx, cols):
        r0 = pl.multiple_of(xx * 8, 8)
        return jnp.concatenate(
            [part[hh, k, 0, pl.ds(r0, 8), cols], part[hh, k, 1, pl.ds(r0, 8), cols]], axis=0
        )

    halves = (slice(0, HW), slice(HW, CW))
    ahead = ((x + 1) % 4, (x + 3) % 4)
    far = (x + 2) % 4

    def project(hh):
        summed = own_keep[hh]
        for d in (4, 3, 5, 2, 6, 1, 7):
            slot = (z + d) % 8
            c_landed(hh, slot)
            summed = summed + c_recv[hh, slot].astype(F32)
        dk = (summed[:, :HD] * SCALE).astype(BF)
        dv = summed[:, HD:].astype(BF)
        o_pdk[hh * HR : (hh + 1) * HR, :] = dk
        o_pdv[hh * HR : (hh + 1) * HR, :] = dv
        both = jnp.concatenate([dk, dv], axis=1)
        for k in range(NCOL):
            for half in range(2):
                rows = slice(half * (D // 2) + k * CW, half * (D // 2) + (k + 1) * CW)
                part[hh, k, half] = dot(both, kvw[rows, :], NT)
            for side in range(2):
                x1_send[hh, k, side, 0] = piece(hh, k, far, halves[side]).astype(BF)
                x1_send[hh, k, side, 1] = piece(hh, k, ahead[side], halves[1 - side]).astype(BF)
                x1_copy(hh, k, side).start()

    def second(hh):
        for k in range(NCOL):
            for side in range(2):
                x1_copy(hh, k, side).wait_recv()
                mine = piece(hh, k, ahead[side], halves[side])
                x2_send[hh, k, side] = (mine + x1_recv[hh, k, side, 0].astype(F32)).astype(BF)
                x2_copy(hh, k, side).start()

    def third(hh):
        for k in range(NCOL):
            for side in range(2):
                x2_copy(hh, k, side).wait_recv()
            for half in range(2):
                got = (
                    piece(hh, k, x, halves[half])
                    + x2_recv[hh, k, half].astype(F32)
                    + x1_recv[hh, k, 1 - half, 1].astype(F32)
                )
                y_keep[hh, k, :, halves[half]] = got
                y_send[hh, k, :, halves[half]] = got.astype(BF)
            pl.when(yh != hh)(lambda: y_copy(hh, k).start())

    project(0)
    roll_queries(0, 2)
    project(1)
    second(0)
    roll_queries(2, 5)
    second(1)
    third(0)
    roll_queries(5, 7)
    third(1)
    roll_queries(7, 8)
    prompt_query(0)
    prompt_query(1)
    for k in range(NCOL):
        y_copy(0, k).wait_recv()
        full = y_keep[yh, k] + y_recv[k].astype(F32)
        o_in[:, k * CW : (k + 1) * CW] = full[0:8].astype(BF)
        o_in[:, D // 2 + k * CW : D // 2 + (k + 1) * CW] = full[8:16].astype(BF)
    for i in range(8):
        a_copy(i).wait_send()
        b_copy(i).wait_send()
        c_copy(i, 0, z).wait_send()
        if i % 4 < 3:
            c_copy(i, 1, z).wait_send()
    for k in range(NCOL):
        for hh in range(2):
            for side in range(2):
                x1_copy(hh, k, side).wait_send()
                x2_copy(hh, k, side).wait_send()
        y_copy(0, k).wait_send()


def hand_on_kernel(*refs):
    count = (len(refs) - 2) // 3
    stage, arrive, leave = refs[2 * count : 3 * count], refs[-2], refs[-1]
    loads = [pltpu.make_async_copy(refs[i], stage[i], arrive.at[i]) for i in range(count)]
    stores = [pltpu.make_async_copy(stage[i], refs[count + i], leave.at[i]) for i in range(count)]
    for cp in loads:
        cp.start()
    for load, store in zip(loads, stores):
        load.wait()
        store.start()
    for cp in stores:
        cp.wait()


def hand_on(arrays):
    spec = pl.BlockSpec(memory_space=pl.ANY)
    count = len(arrays)
    return pl.pallas_call(
        hand_on_kernel,
        in_specs=[spec] * count,
        out_specs=[spec] * count,
        out_shape=[jax.ShapeDtypeStruct(a.shape, a.dtype) for a in arrays],
        scratch_shapes=[pltpu.VMEM(a.shape, a.dtype) for a in arrays]
        + [pltpu.SemaphoreType.DMA((count,))] * 2,
    )(*arrays)


def body(*args):
    anyspec = pl.BlockSpec(memory_space=pl.ANY)
    vspec = pl.BlockSpec(memory_space=pltpu.VMEM)
    sspec = pl.BlockSpec(memory_space=pltpu.SMEM)
    shape = jax.ShapeDtypeStruct
    dma = pltpu.SemaphoreType.DMA
    rows = HEADS * (SR + PR)
    return pl.pallas_call(
        body_kernel,
        in_specs=[anyspec] * 8 + [sspec] + [anyspec] * 2,
        out_specs=[vspec] * 7,
        out_shape=[
            shape((PR, HEADS * HD), BF),
            shape((PR, HD), BF),
            shape((PR, HD), BF),
            shape((1, SR, HEADS * HD), BF),
            shape((1, SR, HD), BF),
            shape((1, SR, HD), BF),
            shape((8, D), BF),
        ],
        scratch_shapes=[
            pltpu.VMEM((ROLL + 4, 2, PR, HD), BF),
            pltpu.VMEM((HD, KEYS + SR), BF),
            pltpu.VMEM((rows, HD), BF),
            pltpu.VMEM((rows, HD), BF),
            pltpu.VMEM((KEYS + SR, rows), BF),
            pltpu.VMEM((KEYS + SR, rows), BF),
            pltpu.VMEM((2, KEYS + SR, SR), F32),
            pltpu.VMEM((2, KEYS + SR, SR), F32),
            pltpu.VMEM((D, 2 * HD), BF),
            pltpu.VMEM((8, 2, 2, HR, 2 * HD), BF),
            pltpu.VMEM((8, 2, 2, HR, 2 * HD), F32),
            pltpu.VMEM((8, 2, 2, HR, 2 * HD), BF),
            pltpu.VMEM((8, 2, HR, 2 * HD), BF),
            pltpu.VMEM((8, 2, HR, 2 * HD), F32),
            pltpu.VMEM((8, 2, HR, 2 * HD), BF),
            pltpu.VMEM((8, 2, HR, 2 * HD), BF),
            pltpu.VMEM((2, 8, HR, 2 * HD), BF),
            pltpu.VMEM((2, HR, 2 * HD), F32),
            pltpu.VMEM((2, NCOL, 2, HR, CW), F32),
            pltpu.VMEM((2, NCOL, 2, 2, 16, HW), BF),
            pltpu.VMEM((2, NCOL, 2, 2, 16, HW), BF),
            pltpu.VMEM((2, NCOL, 2, 16, HW), BF),
            pltpu.VMEM((2, NCOL, 2, 16, HW), BF),
            pltpu.VMEM((2, NCOL, 16, CW), F32),
            pltpu.VMEM((2, NCOL, 16, CW), BF),
            pltpu.VMEM((NCOL, 16, CW), BF),
            dma((44,)),
            dma((31,)),
            dma((32,)),
            dma((8,)),
            dma((8,)),
            dma((8,)),
            dma((8,)),
            dma((8, 2)),
            dma((2, 8)),
            dma((2, NCOL, 2)),
            dma((2, NCOL, 2)),
            dma((2, NCOL, 2)),
            dma((2, NCOL, 2)),
            dma((NCOL,)),
            dma((NCOL,)),
        ],
        compiler_params=pltpu.CompilerParams(
            collective_id=0, has_side_effects=True, vmem_limit_bytes=60 * 1024 * 1024
        ),
    )(*args)


def solution(mesh):
    placed = (
        P("roll", "kv"),
        P("roll", "kv"),
        P("roll", "kv"),
        P("roll", "kv"),
        P("roll", None, "kv"),
        P("roll", None, "kv"),
        P("roll", None, "kv"),
        P("roll", None, "kv"),
        P("roll"),
        P(None, "kv"),
        P(None, "kv"),
    )
    return jax.shard_map(
        lambda *args: tuple(hand_on(body(*args))),
        mesh=mesh,
        in_specs=placed,
        out_specs=(
            P("roll", "kv"),
            P("roll", "kv"),
            P("roll", "kv"),
            P("roll", None, "kv"),
            P("roll", None, "kv"),
            P("roll", None, "kv"),
            P(("roll", "kv"), None),
        ),
        check_vma=False,
    )
```

```python
import functools

import jax
import jax.numpy as jnp
from jax import lax
from jax.experimental import pallas as pl
from jax.experimental.pallas import tpu as pltpu
from jax.sharding import PartitionSpec as P

F32 = jnp.float32
BF = jnp.bfloat16
HD = 128
HEADS = 8
PR = 64
HR = PR // 2
SR = 256
ROLL = 32
KEYS = 2048
CK = 256
SCALE = HD**-0.5
ALPHA = SCALE * 1.4426950408889634
NEG = -1e30
NT = (((1,), (1,)), ((), ()))
NN = (((1,), (0,)), ((), ()))
MESH = pl.DeviceIdType.MESH
D = 8192
NCOL = 2
CW = D // 2 // NCOL
HW = CW // 2
LAG_A = 2
LAG_B = 4


def dot(a, b, dims):
    return lax.dot_general(a, b, dims, preferred_element_type=F32)


def fold(x, op):
    return op(x.reshape(x.shape[0] // 8, 8, x.shape[1]), axis=0)


def body_kernel(
    pq, pk, pv, pdo, sq, sk, sv, sdo, ln, kw_hbm, vw_hbm,
    o_pdq, o_pdk, o_pdv, o_sdq, o_sdk, o_sdv, o_in,
    kv, kt, q, do, ex, dsc, dp_s, s_s, kvw,
    a_send, a_keep, a_recv, b_send, b_keep, b_recv, c_send, c_recv, own_keep,
    part, x1_send, x1_recv, x2_send, x2_recv, y_keep, y_send, y_recv,
    loc, ag_s, ag_r, a_ss, a_rs, b_ss, b_rs, c_ss, c_rs,
    x1_ss, x1_rs, x2_ss, x2_rs, y_ss, y_rs,
):
    roll = lax.axis_index("roll")
    grp = lax.axis_index("kv")
    z = roll // 4
    y = (roll // 2) % 2
    c = roll % 2
    yh = grp // 4
    x = grp % 4

    def rdev(zz, yy, cc):
        return (zz * 4 + yy * 2 + cc, grp)

    def kdev(hh, xx):
        return (roll, hh * 4 + xx)

    sib = rdev(z, y, 1 - c)
    ypar = rdev(z, 1 - y, c)
    xp = kdev(yh, (x + 1) % 4)
    xm = kdev(yh, (x + 3) % 4)
    hpar = kdev(1 - yh, x)

    copies = []

    def local(src, dst):
        cp = pltpu.make_async_copy(src, dst, loc.at[len(copies)])
        cp.start()
        copies.append(cp)

    local(pk, kv.at[roll, 0])
    local(pv, kv.at[roll, 1])
    for h in range(HEADS):
        cols = slice(h * HD, (h + 1) * HD)
        local(sq.at[0, :, cols], q.at[h * SR : (h + 1) * SR, :])
        local(sdo.at[0, :, cols], do.at[h * SR : (h + 1) * SR, :])
        base = HEADS * SR + h * PR
        local(pq.at[:, cols], q.at[base : base + PR, :])
        local(pdo.at[:, cols], do.at[base : base + PR, :])
    for i in range(4):
        local(sk.at[0, i * PR : (i + 1) * PR, :], kv.at[ROLL + i, 0])
        local(sv.at[0, i * PR : (i + 1) * PR, :], kv.at[ROLL + i, 1])
    local(kw_hbm, kvw.at[:, 0:HD])
    local(vw_hbm, kvw.at[:, HD : 2 * HD])

    barrier = pltpu.get_barrier_semaphore()
    peers = [rdev((z + d) % 8, y, c) for d in range(1, 8)] + [sib, ypar, xp, xm, hpar]
    for peer in peers:
        pl.semaphore_signal(barrier, inc=1, device_id=peer, device_id_type=MESH)
    pl.semaphore_wait(barrier, len(peers))

    def gather_copy(block, peer, slot):
        return pltpu.make_async_remote_copy(
            src_ref=kv.at[block], dst_ref=kv.at[block],
            send_sem=ag_s.at[slot], recv_sem=ag_r.at[block],
            device_id=peer, device_id_type=MESH,
        )

    sends = []

    def push(block, peer):
        cp = gather_copy(block, peer, len(sends))
        cp.start()
        sends.append(cp)

    copies[0].wait()
    copies[1].wait()
    order = (1, 7, 2, 6, 3, 5, 4)
    for d in order:
        push(roll, rdev((z + d) % 8, y, c))
    push(roll, ypar)
    push(roll, sib)
    for d in order:
        src = ((z + 8 - d) % 8) * 4 + y * 2 + c
        gather_copy(src, sib, 0).wait_recv()
        push(src, ypar)
        push(src, sib)
    for d in (0,) + order:
        src = ((z + 8 - d) % 8) * 4 + (1 - y) * 2 + c
        gather_copy(src, sib, 0).wait_recv()
        push(src, sib)
    for cp in copies[2:-2]:
        cp.wait()
    for d in (0,) + order:
        for yy in range(2):
            src = ((z + 8 - d) % 8) * 4 + yy * 2 + 1 - c
            gather_copy(src, sib, 0).wait_recv()
    for cp in sends:
        cp.wait_send()

    def keys(i):
        return kv[4 * i : 4 * i + 4, 0].reshape(CK, HD)

    def values(i):
        return kv[4 * i : 4 * i + 4, 1].reshape(CK, HD)

    n_live = ln[0]
    live = lax.broadcasted_iota(jnp.int32, (SR, HD), 0) < n_live
    for h in range(HEADS):
        rows = slice(h * SR, (h + 1) * SR)
        do[rows, :] = jnp.where(live, do[rows, :], jnp.zeros((), BF))
    kpos = lax.broadcasted_iota(jnp.int32, (CK, SR), 0)
    qpos = lax.broadcasted_iota(jnp.int32, (CK, SR), 1)

    def own_mask(i, s):
        if i < 8:
            return s
        return jnp.where((kpos <= qpos) & (kpos < n_live), s, NEG)

    def causal_mask(i, s):
        return jnp.where(kpos + i * CK <= roll * PR + (qpos & (PR - 1)), s, NEG)

    def tile(t, slot, chunks, mask):
        r0 = pl.multiple_of(t * SR, SR)
        cols = pl.ds(r0, SR)
        qt = q[cols, :]
        dt = do[cols, :]
        top = jnp.full((8, SR), NEG, F32)
        for i in range(chunks):
            s = mask(i, dot(keys(i), qt, NT))
            s_s[slot, i * CK : (i + 1) * CK, :] = s
            top = jnp.maximum(top, fold(s, jnp.max))
        yield
        top = jnp.max(top, axis=0, keepdims=True) * ALPHA
        total = jnp.zeros((8, SR), F32)
        delta = jnp.zeros((8, SR), F32)
        for i in range(chunks):
            rows = slice(i * CK, (i + 1) * CK)
            e = jnp.exp2(s_s[slot, rows, :] * ALPHA - top)
            dp = dot(values(i), dt, NT)
            total = total + fold(e, jnp.sum)
            delta = delta + fold(e * dp, jnp.sum)
            s_s[slot, rows, :] = e
            dp_s[slot, rows, :] = dp
        inv = 1.0 / jnp.sum(total, axis=0, keepdims=True)
        delta = jnp.sum(delta, axis=0, keepdims=True) * inv
        yield
        for i in range(chunks):
            rows = slice(i * CK, (i + 1) * CK)
            p = s_s[slot, rows, :] * inv
            ds = (p * (dp_s[slot, rows, :] - delta)).astype(BF)
            ex[rows, cols] = p.astype(BF)
            dsc[rows, cols] = ds
        yield

    def pair(t, chunks, mask):
        tiles = [tile(2 * t + slot, slot, chunks, mask) for slot in range(2)]
        for _ in range(3):
            for one in tiles:
                next(one)

    def roll_pair(t, carry):
        pair(t, 9, own_mask)
        return carry

    lax.fori_loop(0, HEADS // 2, roll_pair, 0)

    def prompt_pair(t, carry):
        pair(t, 8, causal_mask)
        return carry

    lax.fori_loop(HEADS // 2, HEADS // 2 + 1, prompt_pair, 0)

    def turn_keys():
        for i in range(9):
            kt[:, i * CK : (i + 1) * CK] = keys(i).T

    def query_grad(t, rows):
        cols = pl.ds(pl.multiple_of(t * SR, SR), SR)
        return (dot(kt[:, 0:rows], dsc[0:rows, cols], NN) * SCALE).T.astype(BF)

    def roll_query(t, carry):
        o_sdq[0, :, pl.ds(pl.multiple_of(t * HD, HD), HD)] = query_grad(t, KEYS + SR)
        return carry

    def roll_queries(first, last):
        lax.fori_loop(first, last, roll_query, 0)

    def prompt_query(i):
        dq = query_grad(HEADS + i, KEYS)
        for h in range(4):
            o_pdq[:, (4 * i + h) * HD : (4 * i + h + 1) * HD] = dq[h * PR : (h + 1) * PR, :]

    own = slice(KEYS, KEYS + SR)
    live_rows = HEADS * SR

    def zoff(i):
        return (z + 4 + (1 - 2 * (i % 2)) * ((i + 1) // 2)) % 8

    def a_copy(i):
        return pltpu.make_async_remote_copy(
            src_ref=a_send.at[i], dst_ref=a_recv.at[i], send_sem=a_ss.at[i],
            recv_sem=a_rs.at[i], device_id=sib, device_id_type=MESH,
        )

    def b_copy(i):
        return pltpu.make_async_remote_copy(
            src_ref=b_send.at[i], dst_ref=b_recv.at[i], send_sem=b_ss.at[i],
            recv_sem=b_rs.at[i], device_id=ypar, device_id_type=MESH,
        )

    def c_copy(i, zi, zz):
        return pltpu.make_async_remote_copy(
            src_ref=c_send.at[i, zi], dst_ref=c_recv.at[i // 4, z], send_sem=c_ss.at[i, zi],
            recv_sem=c_rs.at[i // 4, z], device_id=rdev(zz, y, c), device_id_type=MESH,
        )

    def c_landed(hh, slot):
        pltpu.make_async_remote_copy(
            src_ref=c_send.at[0, 0], dst_ref=c_recv.at[hh, slot], send_sem=c_ss.at[0, 0],
            recv_sem=c_rs.at[hh, slot], device_id=sib, device_id_type=MESH,
        ).wait_recv()

    first_core = c == 0
    first_y = y == 0

    def compute(i):
        def gather(ref):
            picked = []
            for zi in range(2):
                k0 = zoff(2 * (i % 4) + zi) * CK + (i // 4) * HR
                for b in range(4):
                    picked.append(ref[pl.ds(pl.multiple_of(k0 + b * PR, HR), HR), :])
            return jnp.concatenate(picked, axis=0)

        for part_, g in ((0, dot(gather(dsc), q[...], NN)), (1, dot(gather(ex), do[...], NN))):
            col = slice(part_ * HD, (part_ + 1) * HD)
            for zi in range(2):
                for yy in range(2):
                    r0 = (zi * 4 + yy * 2) * HR
                    lo, hi = g[r0 : r0 + HR], g[r0 + HR : r0 + 2 * HR]
                    a_keep[i, zi, yy, :, col] = jnp.where(first_core, lo, hi)
                    a_send[i, zi, yy, :, col] = jnp.where(first_core, hi, lo).astype(BF)
        a_copy(i).start()

    def after_a(i):
        a_copy(i).wait_recv()
        s0 = a_keep[i, :, 0] + a_recv[i, :, 0].astype(F32)
        s1 = a_keep[i, :, 1] + a_recv[i, :, 1].astype(F32)
        b_keep[i] = jnp.where(first_y, s0, s1)
        b_send[i] = jnp.where(first_y, s1, s0).astype(BF)
        b_copy(i).start()

    def send_c(i):
        b_copy(i).wait_recv()
        both = b_keep[i] + b_recv[i].astype(F32)
        c_send[i] = both.astype(BF)
        c_copy(i, 0, zoff(2 * (i % 4))).start()

        @pl.when(i % 4 < 3)
        def _():
            c_copy(i, 1, zoff(2 * (i % 4) + 1)).start()

        @pl.when(i % 4 == 3)
        def _():
            own_keep[i // 4] = both[1]

    def grads(i, carry):
        compute(i)
        pl.when(i >= LAG_A)(lambda: after_a(i - LAG_A))
        pl.when(i >= LAG_B)(lambda: send_c(i - LAG_B))
        return carry

    lax.fori_loop(0, 8, grads, 0)

    def rest_a(i, carry):
        after_a(i)
        return carry

    def rest_c(i, carry):
        send_c(i)
        return carry

    lax.fori_loop(8 - LAG_A, 8, rest_a, 0)
    lax.fori_loop(8 - LAG_B, 6, rest_c, 0)
    turn_keys()
    o_sdv[0] = dot(ex[own, 0:live_rows], do[0:live_rows, :], NN).astype(BF)
    o_sdk[0] = (dot(dsc[own, 0:live_rows], q[0:live_rows, :], NN) * SCALE).astype(BF)
    lax.fori_loop(6, 8, rest_c, 0)

    copies[-2].wait()
    copies[-1].wait()

    def x_copy(send, recv, ss, rs, hh, k, side):
        return pltpu.make_async_remote_copy(
            src_ref=send.at[hh, k, side], dst_ref=recv.at[hh, k, side],
            send_sem=ss.at[hh, k, side], recv_sem=rs.at[hh, k, side],
            device_id=(xp, xm)[side], device_id_type=MESH,
        )

    def x1_copy(hh, k, side):
        return x_copy(x1_send, x1_recv, x1_ss, x1_rs, hh, k, side)

    def x2_copy(hh, k, side):
        return x_copy(x2_send, x2_recv, x2_ss, x2_rs, hh, k, side)

    def y_copy(hh, k):
        return pltpu.make_async_remote_copy(
            src_ref=y_send.at[hh, k], dst_ref=y_recv.at[k], send_sem=y_ss.at[k],
            recv_sem=y_rs.at[k], device_id=hpar, device_id_type=MESH,
        )

    def piece(hh, k, xx, cols):
        r0 = pl.multiple_of(xx * 8, 8)
        return jnp.concatenate(
            [part[hh, k, 0, pl.ds(r0, 8), cols], part[hh, k, 1, pl.ds(r0, 8), cols]], axis=0
        )

    halves = (slice(0, HW), slice(HW, CW))
    ahead = ((x + 1) % 4, (x + 3) % 4)
    far = (x + 2) % 4

    def project(hh):
        summed = own_keep[hh]
        for d in (4, 3, 5, 2, 6, 1, 7):
            slot = (z + d) % 8
            c_landed(hh, slot)
            summed = summed + c_recv[hh, slot].astype(F32)
        dk = (summed[:, :HD] * SCALE).astype(BF)
        dv = summed[:, HD:].astype(BF)
        o_pdk[hh * HR : (hh + 1) * HR, :] = dk
        o_pdv[hh * HR : (hh + 1) * HR, :] = dv
        both = jnp.concatenate([dk, dv], axis=1)
        for k in range(NCOL):
            for half in range(2):
                rows = slice(half * (D // 2) + k * CW, half * (D // 2) + (k + 1) * CW)
                part[hh, k, half] = dot(both, kvw[rows, :], NT)
            for side in range(2):
                x1_send[hh, k, side, 0] = piece(hh, k, far, halves[side]).astype(BF)
                x1_send[hh, k, side, 1] = piece(hh, k, ahead[side], halves[1 - side]).astype(BF)
                x1_copy(hh, k, side).start()

    def second(hh):
        for k in range(NCOL):
            for side in range(2):
                x1_copy(hh, k, side).wait_recv()
                mine = piece(hh, k, ahead[side], halves[side])
                x2_send[hh, k, side] = (mine + x1_recv[hh, k, side, 0].astype(F32)).astype(BF)
                x2_copy(hh, k, side).start()

    def third(hh):
        for k in range(NCOL):
            for side in range(2):
                x2_copy(hh, k, side).wait_recv()
            for half in range(2):
                got = (
                    piece(hh, k, x, halves[half])
                    + x2_recv[hh, k, half].astype(F32)
                    + x1_recv[hh, k, 1 - half, 1].astype(F32)
                )
                y_keep[hh, k, :, halves[half]] = got
                y_send[hh, k, :, halves[half]] = got.astype(BF)
            pl.when(yh != hh)(lambda: y_copy(hh, k).start())

    project(0)
    roll_queries(0, 2)
    project(1)
    second(0)
    roll_queries(2, 5)
    second(1)
    third(0)
    roll_queries(5, 7)
    third(1)
    roll_queries(7, 8)
    prompt_query(0)
    prompt_query(1)
    for k in range(NCOL):
        y_copy(0, k).wait_recv()
        full = y_keep[yh, k] + y_recv[k].astype(F32)
        o_in[:, k * CW : (k + 1) * CW] = full[0:8].astype(BF)
        o_in[:, D // 2 + k * CW : D // 2 + (k + 1) * CW] = full[8:16].astype(BF)
    for i in range(8):
        a_copy(i).wait_send()
        b_copy(i).wait_send()
        c_copy(i, 0, z).wait_send()
        if i % 4 < 3:
            c_copy(i, 1, z).wait_send()
    for k in range(NCOL):
        for hh in range(2):
            for side in range(2):
                x1_copy(hh, k, side).wait_send()
                x2_copy(hh, k, side).wait_send()
        y_copy(0, k).wait_send()


def hand_on_kernel(*refs):
    count = (len(refs) - 2) // 3
    stage, arrive, leave = refs[2 * count : 3 * count], refs[-2], refs[-1]
    loads = [pltpu.make_async_copy(refs[i], stage[i], arrive.at[i]) for i in range(count)]
    stores = [pltpu.make_async_copy(stage[i], refs[count + i], leave.at[i]) for i in range(count)]
    for cp in loads:
        cp.start()
    for load, store in zip(loads, stores):
        load.wait()
        store.start()
    for cp in stores:
        cp.wait()


def hand_on(arrays):
    spec = pl.BlockSpec(memory_space=pl.ANY)
    count = len(arrays)
    return pl.pallas_call(
        hand_on_kernel,
        in_specs=[spec] * count,
        out_specs=[spec] * count,
        out_shape=[jax.ShapeDtypeStruct(a.shape, a.dtype) for a in arrays],
        scratch_shapes=[pltpu.VMEM(a.shape, a.dtype) for a in arrays]
        + [pltpu.SemaphoreType.DMA((count,))] * 2,
    )(*arrays)


def body(*args):
    anyspec = pl.BlockSpec(memory_space=pl.ANY)
    vspec = pl.BlockSpec(memory_space=pltpu.VMEM)
    sspec = pl.BlockSpec(memory_space=pltpu.SMEM)
    shape = jax.ShapeDtypeStruct
    dma = pltpu.SemaphoreType.DMA
    rows = HEADS * (SR + PR)
    return pl.pallas_call(
        body_kernel,
        in_specs=[anyspec] * 8 + [sspec] + [anyspec] * 2,
        out_specs=[vspec] * 7,
        out_shape=[
            shape((PR, HEADS * HD), BF),
            shape((PR, HD), BF),
            shape((PR, HD), BF),
            shape((1, SR, HEADS * HD), BF),
            shape((1, SR, HD), BF),
            shape((1, SR, HD), BF),
            shape((8, D), BF),
        ],
        scratch_shapes=[
            pltpu.VMEM((ROLL + 4, 2, PR, HD), BF),
            pltpu.VMEM((HD, KEYS + SR), BF),
            pltpu.VMEM((rows, HD), BF),
            pltpu.VMEM((rows, HD), BF),
            pltpu.VMEM((KEYS + SR, rows), BF),
            pltpu.VMEM((KEYS + SR, rows), BF),
            pltpu.VMEM((2, KEYS + SR, SR), F32),
            pltpu.VMEM((2, KEYS + SR, SR), F32),
            pltpu.VMEM((D, 2 * HD), BF),
            pltpu.VMEM((8, 2, 2, HR, 2 * HD), BF),
            pltpu.VMEM((8, 2, 2, HR, 2 * HD), F32),
            pltpu.VMEM((8, 2, 2, HR, 2 * HD), BF),
            pltpu.VMEM((8, 2, HR, 2 * HD), BF),
            pltpu.VMEM((8, 2, HR, 2 * HD), F32),
            pltpu.VMEM((8, 2, HR, 2 * HD), BF),
            pltpu.VMEM((8, 2, HR, 2 * HD), BF),
            pltpu.VMEM((2, 8, HR, 2 * HD), BF),
            pltpu.VMEM((2, HR, 2 * HD), F32),
            pltpu.VMEM((2, NCOL, 2, HR, CW), F32),
            pltpu.VMEM((2, NCOL, 2, 2, 16, HW), BF),
            pltpu.VMEM((2, NCOL, 2, 2, 16, HW), BF),
            pltpu.VMEM((2, NCOL, 2, 16, HW), BF),
            pltpu.VMEM((2, NCOL, 2, 16, HW), BF),
            pltpu.VMEM((2, NCOL, 16, CW), F32),
            pltpu.VMEM((2, NCOL, 16, CW), BF),
            pltpu.VMEM((NCOL, 16, CW), BF),
            dma((44,)),
            dma((31,)),
            dma((32,)),
            dma((8,)),
            dma((8,)),
            dma((8,)),
            dma((8,)),
            dma((8, 2)),
            dma((2, 8)),
            dma((2, NCOL, 2)),
            dma((2, NCOL, 2)),
            dma((2, NCOL, 2)),
            dma((2, NCOL, 2)),
            dma((NCOL,)),
            dma((NCOL,)),
        ],
        compiler_params=pltpu.CompilerParams(
            collective_id=0, has_side_effects=True, vmem_limit_bytes=60 * 1024 * 1024
        ),
    )(*args)


def solution(mesh):
    placed = (
        P("roll", "kv"),
        P("roll", "kv"),
        P("roll", "kv"),
        P("roll", "kv"),
        P("roll", None, "kv"),
        P("roll", None, "kv"),
        P("roll", None, "kv"),
        P("roll", None, "kv"),
        P("roll"),
        P(None, "kv"),
        P(None, "kv"),
    )
    return jax.shard_map(
        lambda *args: tuple(hand_on(body(*args))),
        mesh=mesh,
        in_specs=placed,
        out_specs=(
            P("roll", "kv"),
            P("roll", "kv"),
            P("roll", "kv"),
            P("roll", None, "kv"),
            P("roll", None, "kv"),
            P("roll", None, "kv"),
            P(("roll", "kv"), None),
        ),
        check_vma=False,
    )
```
